256 devices in a mesh: row: 16 (over z, x_hi), col: 8 (over y, x_lo), layer: 2 (over core).
Axes of the slice: x: 4 (x_hi: 2, x_lo: 2; x = x_hi * 2 + x_lo), y: 4, z: 8, core: 2. Of those that a mesh axis runs over, the one named last changes fastest.
Arguments:
- t_amps: float32 [512, 131072], P('col', ('row', 'layer')), may hold values from -6 to 6
- v_tiles: float32 [16, 2, 16, 16, 4096], P('col', 'layer', 'row'), may hold values from -0.09375 to 0.09375
- v_where: int32 [16, 2, 16, 16], P('col', 'layer', 'row'), may hold values from -1 to 255, as said below
Outputs:
- residual_block: float32 [512, 4096], P('col', ('row', 'layer'))
The draws below stay inside these ranges and needn't reach their ends.
Inputs may be any that keep to these rules, and one draw needn't show every extreme that they name: Within each list v_where[j, l, r, :] the live positions are distinct and come first, the unused slots (-1) after them; some list in every draw has all 16 slots live, and every list has at least one.
All inputs are finite; a program needn't handle non-finite values.
Results may differ from the reference program's by a relative error of at most 0.0003.
Values sent between devices are 32-bit elements; how exact they have to be, the bound alone decides.
No kernel may reach another device: no remote copies, remote signals or barrier semaphores. Data moves between devices by JAX's collectives and lax.ppermute only.
A program may use at most 64 MiB of HBM per device.

```python
import jax
import jax.numpy as jnp
from jax import lax

TILE = 64
CD = 131072
AB_DEV = 128
IJ = 512
CDT = 64
ABT = 4
CAP = 16
N_ROW = 16
N_LAYER = 2


def draw_v_where(key, part):
    key = jax.random.fold_in(key, 7)
    list_count = N_ROW * N_LAYER * N_ROW
    key_pos, key_count, key_full = jax.random.split(key, 3)
    pos_keys = jax.random.split(key_pos, list_count)
    positions = jax.vmap(lambda one_key: jax.random.permutation(one_key, CDT * ABT)[:CAP])(pos_keys)
    fewest = max(1, CAP // 4)
    levels = jax.random.randint(key_count, (list_count,), 0, 256)
    counts = fewest + (CAP - fewest + 1) * levels * levels // 65536
    fullest = jax.random.randint(key_full, (), 0, list_count)
    counts = jnp.where(jnp.arange(list_count) == fullest, CAP, counts)
    slot_ids = jnp.arange(CAP)
    spots_out = jnp.where(slot_ids[None, :] < counts[:, None], positions, -1)
    return spots_out.reshape(N_ROW, N_LAYER, N_ROW, CAP).astype(jnp.int32)


def block_scale(stream_key, extent, cuts, low, top_value):
    gain, own = 1.0, jax.random.fold_in(stream_key, 6)
    for dim, shards_of in cuts:
        steps = jnp.exp(jax.random.uniform(jax.random.fold_in(own, dim), (shards_of,), jnp.float32, low / len(cuts), top_value / len(cuts)))
        gain = gain * jnp.repeat(steps, extent[dim] // shards_of).reshape([-1 if axis == dim else 1 for axis in range(len(extent))])
    return gain


def scatter_about(key, extent, spread, limit, cuts=(), kind=jnp.bfloat16):
    entries = spread * jax.random.normal(key, extent, jnp.float32)
    if cuts:
        entries = entries * block_scale(key, extent, cuts, -0.22, 0.18)
    return jnp.clip(entries, -limit, limit).astype(kind)


def setup_inputs(seed: int = 0) -> dict:
    streams_of = jax.random.split(jax.random.key(seed), 4)
    t_amps = scatter_about(streams_of[0], (IJ, CD), 1.0, 6.0, ((0, 8), (1, 32)), jnp.float32)
    v_tiles = scatter_about(streams_of[1], (N_ROW, N_LAYER, N_ROW, CAP, TILE * TILE), (CD // 32) ** -0.5, 0.09375, ((0, 8), (1, 2), (2, 16)), jnp.float32)
    v_where = draw_v_where(jax.random.fold_in(streams_of[3], 71), 0)
    return dict(t_amps=t_amps, v_tiles=v_tiles, v_where=v_where)


def reference(t_amps, v_tiles, v_where):
    ij_rows = t_amps.shape[0]
    fine_count = v_tiles.shape[0] * v_tiles.shape[1]
    row_blocks = v_tiles.shape[2]
    slot_count = v_tiles.shape[3]
    block_cols = t_amps.shape[1] // fine_count
    cd_tiles = block_cols // TILE
    ab_tiles = AB_DEV * N_LAYER // TILE
    all_tiles = v_tiles.reshape(fine_count, row_blocks, slot_count, TILE, TILE)
    all_spots = v_where.reshape(fine_count, row_blocks, slot_count)

    def per_fine(totals, fine_id):
        start = (fine_id * block_cols).astype(jnp.int32)
        t_block = lax.dynamic_slice_in_dim(t_amps, start, block_cols, 1).reshape(ij_rows, cd_tiles, TILE)
        v_mats = lax.dynamic_index_in_dim(all_tiles, fine_id, 0, keepdims=False)
        v_spots = lax.dynamic_index_in_dim(all_spots, fine_id, 0, keepdims=False)
        is_live = v_spots >= 0
        v_safe = jnp.maximum(v_spots, 0)
        cd_tile = v_safe // ab_tiles
        ab_tile = v_safe % ab_tiles
        picked = jnp.take(t_block, cd_tile.reshape(-1), axis=1).reshape(ij_rows, row_blocks, slot_count, TILE)
        product = jnp.einsum("iptc,ptca->ipta", picked, v_mats, precision=lax.Precision.HIGHEST)
        onehot = ((ab_tile[..., None] == jnp.arange(ab_tiles, dtype=jnp.int32)) & is_live[..., None]).astype(jnp.float32)
        t_added = jnp.einsum("ipta,ptb->ipba", product, onehot, precision=lax.Precision.HIGHEST)
        return totals + t_added, None

    initial = jnp.zeros((ij_rows, row_blocks, ab_tiles, TILE), jnp.float32)
    totals, _ = lax.scan(per_fine, initial, jnp.arange(fine_count, dtype=jnp.int32))
    return totals.reshape(ij_rows, row_blocks * ab_tiles * TILE)
```

```python
import jax
import jax.numpy as jnp
from jax import lax
from jax.experimental import pallas as pl
from jax.experimental.pallas import tpu as pltpu
from jax.sharding import PartitionSpec as P

TILE = 64
AB_DEV = 128
LANES = 128
HALF = TILE // 2


def split_rows(x):
    hi = x.astype(jnp.bfloat16)
    return hi, (x - hi.astype(jnp.float32)).astype(jnp.bfloat16)


def contract_kernel(spots_ref, t_ref, v_ref, out_ref, t_tiles, lhs, rhs):
    ij = t_ref.shape[0]
    pair = v_ref.shape[1] // HALF
    slots = v_ref.shape[0] * pair
    block = pl.program_id(0)

    @pl.when(block == 0)
    def _():
        row = lax.broadcasted_iota(jnp.int32, (LANES, 2 * LANES), 0)
        col = lax.broadcasted_iota(jnp.int32, (LANES, 2 * LANES), 1)
        source = (col // LANES) * TILE + 2 * (col % HALF) + (col % TILE) // HALF
        pick = (row == source).astype(jnp.bfloat16)
        for at in range(t_ref.shape[1] // LANES):
            hi, lo = split_rows(t_ref[:, at * LANES : (at + 1) * LANES])
            both = jnp.dot(
                jnp.concatenate([hi, lo], axis=0), pick, preferred_element_type=jnp.float32
            ).astype(jnp.bfloat16)
            t_tiles[2 * at] = both[:, :LANES]
            t_tiles[2 * at + 1] = both[:, LANES:]

    lane_half = lax.broadcasted_iota(jnp.int32, (HALF, LANES), 1) // TILE
    for t in range(slots):
        spot = spots_ref[block, t]
        live = spot >= 0
        safe = jnp.maximum(spot, 0)
        ab_half = safe & 1
        ab_pair = (safe >> 1) & 1
        lhs[:, t * LANES : (t + 1) * LANES] = t_tiles[safe >> 2]
        at = t % pair * HALF
        v = v_ref[t // pair, at : at + HALF]
        swapped = pltpu.roll(v, TILE, 1)
        upper = ab_half == 1
        even = jnp.where(upper, swapped, v)
        odd = jnp.where(upper, v, swapped)
        keep = (lane_half == ab_half) & live
        hi_e, lo_e = split_rows(jnp.where(keep, even, 0.0))
        hi_o, lo_o = split_rows(jnp.where(keep, odd, 0.0))
        rows = jnp.concatenate([hi_e, hi_o, lo_e, lo_o], axis=0)
        none = jnp.zeros_like(rows)
        rhs[t * LANES : (t + 1) * LANES, :LANES] = jnp.where(ab_pair == 0, rows, none)
        rhs[t * LANES : (t + 1) * LANES, LANES:] = jnp.where(ab_pair == 1, rows, none)
    total = jnp.dot(lhs[...], rhs[...], preferred_element_type=jnp.float32)
    total = total[:ij] + total[ij:]
    out_ref[0, 0] = total[:, :LANES]
    out_ref[1, 0] = total[:, LANES:]


def contract(t_block, shares, spots):
    ij, cd = t_block.shape
    blocks, slots = spots.shape
    cols = shares.shape[0]
    rows = slots // cols * HALF
    return pl.pallas_call(
        contract_kernel,
        out_shape=jax.ShapeDtypeStruct((2, blocks, ij, LANES), jnp.float32),
        grid_spec=pltpu.PrefetchScalarGridSpec(
            num_scalar_prefetch=1,
            grid=(blocks,),
            in_specs=[
                pl.BlockSpec((ij, cd), lambda i, _: (0, 0)),
                pl.BlockSpec((cols, rows, LANES), lambda i, _: (0, i, 0)),
            ],
            out_specs=pl.BlockSpec((2, 1, ij, LANES), lambda i, _: (0, i, 0, 0)),
            scratch_shapes=[
                pltpu.VMEM((cd // TILE, 2 * ij, LANES), jnp.bfloat16),
                pltpu.VMEM((2 * ij, slots * LANES), jnp.bfloat16),
                pltpu.VMEM((slots * LANES, 2 * LANES), jnp.bfloat16),
            ],
        ),
        compiler_params=pltpu.CompilerParams(vmem_limit_bytes=32 * 2**20),
        cost_estimate=pl.CostEstimate(
            flops=2 * blocks * 2 * ij * slots * LANES * 2 * LANES,
            bytes_accessed=6 * 2**20,
            transcendentals=0,
        ),
    )(spots, t_block, shares)


def on_device(t_amps, v_tiles, v_where):
    cols = lax.axis_size("col")
    blocks = lax.axis_size("row")
    held, slots = v_tiles.shape[0], v_tiles.shape[3]
    pair = slots // cols
    rows = pair * HALF

    tiles = v_tiles.reshape(held, cols, rows, LANES)
    spots = v_where.reshape(held, cols, 1, pair).astype(jnp.float32)
    spots = jnp.pad(spots, ((0, 0), (0, 0), (0, 7), (0, LANES - pair)))
    parts = jnp.concatenate([tiles, spots], axis=2).transpose(1, 0, 2, 3)
    parts = lax.all_to_all(parts, "col", 0, 0, tiled=True)
    parts = parts.reshape(held * cols, rows + 8, LANES)
    parts = lax.all_to_all(parts, "row", 0, 0, tiled=True)

    spots = jnp.pad(parts[:, rows, :pair].reshape(1, blocks * pair), ((0, 7), (0, LANES - blocks * pair)))
    share = jnp.concatenate([parts[:, :rows].reshape(blocks * rows, LANES), spots], axis=0)
    shares = jnp.broadcast_to(share, (cols, *share.shape))
    shares = lax.all_to_all(shares, "col", 0, 0, tiled=True)
    spots = shares[:, blocks * rows, : blocks * pair].astype(jnp.int32)
    spots = spots.reshape(cols, blocks, pair).transpose(1, 0, 2).reshape(blocks, slots)

    sums = contract(t_amps, shares, spots)
    sums = lax.all_to_all(sums, "layer", 0, 0, tiled=True)
    sums = sums[0] + sums[1]
    sums = lax.all_to_all(sums, "row", 0, 0, tiled=True)
    return jnp.sum(sums, axis=0)


def solution(mesh):
    return jax.shard_map(
        on_device,
        mesh=mesh,
        in_specs=(
            P("col", ("row", "layer")),
            P("col", "layer", "row", None, None),
            P("col", "layer", "row", None),
        ),
        out_specs=P("col", ("row", "layer")),
        check_vma=False,
    )
```

```python
import jax
import jax.numpy as jnp
from jax import lax
from jax.experimental import pallas as pl
from jax.experimental.pallas import tpu as pltpu
from jax.sharding import PartitionSpec as P

TILE = 64
AB_DEV = 128
LANES = 128
HALF = TILE // 2
VMEM = pl.BlockSpec(memory_space=pltpu.VMEM)
SMEM = pl.BlockSpec(memory_space=pltpu.SMEM)


def split_rows(x):
    hi = x.astype(jnp.bfloat16)
    return hi, (x - hi.astype(jnp.float32)).astype(jnp.bfloat16)


def prepare_kernel(t_ref, t_tiles):
    row = lax.broadcasted_iota(jnp.int32, (LANES, 2 * LANES), 0)
    col = lax.broadcasted_iota(jnp.int32, (LANES, 2 * LANES), 1)
    source = (col // LANES) * TILE + 2 * (col % HALF) + (col % TILE) // HALF
    pick = (row == source).astype(jnp.bfloat16)
    for at in range(t_ref.shape[1] // LANES):
        hi, lo = split_rows(t_ref[:, at * LANES : (at + 1) * LANES])
        both = jnp.dot(
            jnp.concatenate([hi, lo], axis=0), pick, preferred_element_type=jnp.float32
        ).astype(jnp.bfloat16)
        t_tiles[2 * at] = both[:, :LANES]
        t_tiles[2 * at + 1] = both[:, LANES:]


def prepare(t_block):
    ij, cd = t_block.shape
    return pl.pallas_call(
        prepare_kernel,
        out_shape=jax.ShapeDtypeStruct((cd // TILE, 2 * ij, LANES), jnp.bfloat16),
        in_specs=[VMEM],
        out_specs=VMEM,
        compiler_params=pltpu.CompilerParams(vmem_limit_bytes=32 * 2**20),
        cost_estimate=pl.CostEstimate(flops=2 * 2 * ij * cd * 2 * LANES, bytes_accessed=3 * 2**20, transcendentals=0),
    )(t_block)


def slot_rows(v, spot):
    lane_half = lax.broadcasted_iota(jnp.int32, (HALF, LANES), 1) // TILE
    safe = jnp.maximum(spot, 0)
    ab_half = safe & 1
    ab_pair = (safe >> 1) & 1
    swapped = pltpu.roll(v, TILE, 1)
    upper = ab_half == 1
    keep = (lane_half == ab_half) & (spot >= 0)
    hi_e, lo_e = split_rows(jnp.where(keep, jnp.where(upper, swapped, v), 0.0))
    hi_o, lo_o = split_rows(jnp.where(keep, jnp.where(upper, v, swapped), 0.0))
    rows = jnp.concatenate([hi_e, hi_o, lo_e, lo_o], axis=0)
    none = jnp.zeros_like(rows)
    return jnp.where(ab_pair == 0, rows, none), jnp.where(ab_pair == 1, rows, none)


def contract_kernel(sources, fresh, pair, *refs):
    count = len(sources)
    starts = [first for first, _, _ in sources]
    place, spots, t_tiles = refs[:3]
    shares = refs[3 : 3 + count]
    if fresh:
        sums = None
        out, lhs, rhs = refs[3 + count :]
    else:
        sums, out, lhs, rhs = refs[3 + count :]
    layer = place[1]
    ij = out.shape[2]
    rows = pair * HALF
    cols = spots.shape[1] // pair
    columns = [((place[0] + shift) & (cols - 1)) ^ flip for _, shift, flip in sources]
    blocks = out.shape[1]
    for block in range(blocks):
        used = [
            n for n in range(count)
            if starts[n] <= block < starts[n] + shares[n].shape[0] // rows
        ]
        buffer = block % 2
        width = len(used) * pair * LANES
        for m, n in enumerate(used):
            base = (block - starts[n]) * rows
            for p in range(pair):
                spot = spots[block, columns[n] * pair + p]
                at = (m * pair + p) * LANES
                lhs[buffer, :, at : at + LANES] = t_tiles[jnp.maximum(spot, 0) >> 2]
                left, right = slot_rows(shares[n][base + p * HALF : base + (p + 1) * HALF], spot)
                rhs[buffer, at : at + LANES, :LANES] = left
                rhs[buffer, at : at + LANES, LANES:] = right
        total = jnp.dot(lhs[buffer, :, :width], rhs[buffer, :width], preferred_element_type=jnp.float32)
        total = total[:ij] + total[ij:]
        mine = total[:, :LANES]
        other = total[:, LANES:]
        if sums is not None:
            mine = mine + sums[layer, block]
            other = other + sums[1 - layer, block]
        out[layer, block] = mine
        out[1 - layer, block] = other


def contract(sums, t_tiles, spots, place, shares, pair):
    blocks = spots.shape[0]
    ij = t_tiles.shape[1] // 2
    sources = tuple(source for source, _ in shares)
    depth = len(shares) * pair * LANES
    given = [place, spots, t_tiles, *(share for _, share in shares)]
    specs = [SMEM, SMEM] + [VMEM] * (1 + len(shares))
    if sums is not None:
        given.append(sums)
        specs.append(VMEM)

    def kernel(*refs):
        contract_kernel(sources, sums is None, pair, *refs)

    return pl.pallas_call(
        kernel,
        out_shape=jax.ShapeDtypeStruct((2, blocks, ij, LANES), jnp.float32),
        in_specs=specs,
        out_specs=VMEM,
        scratch_shapes=[
            pltpu.VMEM((2, 2 * ij, depth), jnp.bfloat16),
            pltpu.VMEM((2, depth, 2 * LANES), jnp.bfloat16),
        ],
        input_output_aliases={} if sums is None else {len(given) - 1: 0},
        compiler_params=pltpu.CompilerParams(vmem_limit_bytes=32 * 2**20),
        cost_estimate=pl.CostEstimate(
            flops=2 * blocks * 2 * ij * depth * 2 * LANES,
            bytes_accessed=(len(shares) + 4) * 2**19,
            transcendentals=0,
        ),
    )(*given)


def on_device(t_amps, v_tiles, v_where):
    cols = lax.axis_size("col")
    blocks = lax.axis_size("row")
    held, slots = v_tiles.shape[0], v_tiles.shape[3]
    pair = slots // cols
    rows = pair * HALF
    place = jnp.stack([lax.axis_index("col"), lax.axis_index("layer")])

    tiles = v_tiles.reshape(held, cols, rows, LANES)
    spots = v_where.reshape(held, 1, 1, slots).astype(jnp.float32)
    spots = jnp.pad(spots, ((0, 0), (0, 0), (0, 7), (0, LANES - slots)))
    spots = jnp.broadcast_to(spots, (held, cols, 8, LANES))
    parts = jnp.concatenate([tiles, spots], axis=2).transpose(1, 0, 2, 3)
    parts = parts.reshape(cols, held * (rows + 8), LANES)
    parts = lax.all_to_all(parts, "col", 0, 0, tiled=True)
    parts = parts.reshape(held * cols, rows + 8, LANES)
    parts = lax.all_to_all(parts, "row", 0, 0, tiled=True)
    spots = parts[:, rows, :slots].astype(jnp.int32)
    own = parts[:, :rows].reshape(blocks * rows, LANES)

    def send(share, to):
        return lax.ppermute(share, "col", [(i, to(i)) for i in range(cols)])

    def up(i):
        return (i + 2) % cols

    def down(i):
        return (i - 2) % cols

    def across(i):
        return i ^ 1

    half = blocks * rows // 2
    partner = send(own, across)
    below = send(own, up)
    above = send(own, down)
    far_low = send(below[:half], up)
    far_high = send(above[half:], down)
    partner_below = send(partner, up)
    partner_above = send(partner, down)
    partner_far_low = send(far_low, across)
    partner_far_high = send(far_high, across)

    t_tiles = prepare(t_amps)

    def add(sums, *shares):
        return contract(sums, t_tiles, spots, place, shares, pair)

    middle = blocks // 2
    sums = add(None, ((0, 0, 0), own))
    sums = add(sums, ((0, 0, 1), partner), ((0, -2, 0), below), ((0, 2, 0), above))
    sums = add(
        sums,
        ((0, -2, 1), partner_below),
        ((0, 2, 1), partner_above),
        ((0, 4, 0), far_low),
        ((middle, 4, 0), far_high),
    )
    sums = add(sums, ((0, 4, 1), partner_far_low), ((middle, 4, 1), partner_far_high))
    sums = sums[0] + lax.ppermute(sums[1], "layer", [(0, 1), (1, 0)])
    sums = lax.all_to_all(sums, "row", 0, 0, tiled=True)
    return jnp.sum(sums, axis=0)


def solution(mesh):
    return jax.shard_map(
        on_device,
        mesh=mesh,
        in_specs=(
            P("col", ("row", "layer")),
            P("col", "layer", "row", None, None),
            P("col", "layer", "row", None),
        ),
        out_specs=P("col", ("row", "layer")),
        check_vma=False,
    )
```

```python
import jax
import jax.numpy as jnp
from jax import lax
from jax.experimental import pallas as pl
from jax.experimental.pallas import tpu as pltpu
from jax.sharding import PartitionSpec as P

TILE = 64
AB_DEV = 128
LANES = 128
HALF = TILE // 2
VMEM = pl.BlockSpec(memory_space=pltpu.VMEM)
SMEM = pl.BlockSpec(memory_space=pltpu.SMEM)


def split_rows(x):
    hi = x.astype(jnp.bfloat16)
    return hi, (x - hi.astype(jnp.float32)).astype(jnp.bfloat16)


def pack_kernel(spots, lists, out):
    held, slots = spots.shape
    cols = out.shape[0]
    pair = slots // cols
    rows = pair * HALF
    lane = lax.broadcasted_iota(jnp.int32, (8, LANES), 1)
    for b in range(held):
        row = jnp.zeros((8, LANES), jnp.float32)
        for s in range(slots):
            row = jnp.where(lane == s, spots[b, s].astype(jnp.float32), row)
        base = b * (rows + 8)
        for c in range(cols):
            for p in range(pair):
                s = c * pair + p
                out[c, base + p * HALF : base + (p + 1) * HALF] = lists[b, s // 8, pl.ds(s % 8, HALF, stride=8), :]
            out[c, base + rows : base + rows + 8] = row


def pack(v_tiles, v_where, cols):
    held, slots = v_tiles.shape[0], v_tiles.shape[3]
    lists = v_tiles.reshape(held, slots // 8, 8, HALF, LANES).transpose(0, 1, 3, 2, 4)
    lists = lists.reshape(held, slots // 8, HALF * 8, LANES)
    return pl.pallas_call(
        pack_kernel,
        out_shape=jax.ShapeDtypeStruct((cols, held * (slots // cols * HALF + 8), LANES), jnp.float32),
        in_specs=[SMEM, VMEM],
        out_specs=VMEM,
        compiler_params=pltpu.CompilerParams(vmem_limit_bytes=16 * 2**20),
        cost_estimate=pl.CostEstimate(flops=0, bytes_accessed=2**20, transcendentals=0),
    )(v_where.reshape(held, slots), lists)


def prepare_kernel(t_ref, t_tiles):
    row = lax.broadcasted_iota(jnp.int32, (LANES, 2 * LANES), 0)
    col = lax.broadcasted_iota(jnp.int32, (LANES, 2 * LANES), 1)
    source = (col // LANES) * TILE + 2 * (col % HALF) + (col % TILE) // HALF
    pick = (row == source).astype(jnp.bfloat16)
    for at in range(t_ref.shape[1] // LANES):
        hi, lo = split_rows(t_ref[:, at * LANES : (at + 1) * LANES])
        both = jnp.dot(
            jnp.concatenate([hi, lo], axis=0), pick, preferred_element_type=jnp.float32
        ).astype(jnp.bfloat16)
        t_tiles[2 * at] = both[:, :LANES]
        t_tiles[2 * at + 1] = both[:, LANES:]


def prepare(t_block):
    ij, cd = t_block.shape
    return pl.pallas_call(
        prepare_kernel,
        out_shape=jax.ShapeDtypeStruct((cd // TILE, 2 * ij, LANES), jnp.bfloat16),
        in_specs=[VMEM],
        out_specs=VMEM,
        compiler_params=pltpu.CompilerParams(vmem_limit_bytes=32 * 2**20),
        cost_estimate=pl.CostEstimate(flops=2 * 2 * ij * cd * 2 * LANES, bytes_accessed=3 * 2**20, transcendentals=0),
    )(t_block)


def slot_rows(v, spot):
    lane_half = lax.broadcasted_iota(jnp.int32, (HALF, LANES), 1) // TILE
    safe = jnp.maximum(spot, 0)
    ab_half = safe & 1
    ab_pair = (safe >> 1) & 1
    swapped = pltpu.roll(v, TILE, 1)
    upper = ab_half == 1
    keep = (lane_half == ab_half) & (spot >= 0)
    hi_e, lo_e = split_rows(jnp.where(keep, jnp.where(upper, swapped, v), 0.0))
    hi_o, lo_o = split_rows(jnp.where(keep, jnp.where(upper, v, swapped), 0.0))
    rows = jnp.concatenate([hi_e, hi_o, lo_e, lo_o], axis=0)
    none = jnp.zeros_like(rows)
    return jnp.where(ab_pair == 0, rows, none), jnp.where(ab_pair == 1, rows, none)


def contract_kernel(sources, fresh, pair, *refs):
    count = len(sources)
    starts = [first for first, _, _ in sources]
    place, spots, t_tiles = refs[:3]
    shares = refs[3 : 3 + count]
    if fresh:
        sums = None
        out, lhs, rhs = refs[3 + count :]
    else:
        sums, out, lhs, rhs = refs[3 + count :]
    layer = place[1]
    ij = out.shape[2]
    rows = pair * HALF
    cols = spots.shape[1] // pair
    columns = [((place[0] + shift) & (cols - 1)) ^ flip for _, shift, flip in sources]
    blocks = out.shape[1]
    for block in range(blocks):
        used = [
            n for n in range(count)
            if starts[n] <= block < starts[n] + shares[n].shape[0] // rows
        ]
        buffer = block % 2
        width = len(used) * pair * LANES
        for m, n in enumerate(used):
            base = (block - starts[n]) * rows
            for p in range(pair):
                spot = spots[block, columns[n] * pair + p]
                at = (m * pair + p) * LANES
                lhs[buffer, :, at : at + LANES] = t_tiles[jnp.maximum(spot, 0) >> 2]
                left, right = slot_rows(shares[n][base + p * HALF : base + (p + 1) * HALF], spot)
                rhs[buffer, at : at + LANES, :LANES] = left
                rhs[buffer, at : at + LANES, LANES:] = right
        total = jnp.dot(lhs[buffer, :, :width], rhs[buffer, :width], preferred_element_type=jnp.float32)
        total = total[:ij] + total[ij:]
        mine = total[:, :LANES]
        other = total[:, LANES:]
        if sums is not None:
            mine = mine + sums[layer, block]
            other = other + sums[1 - layer, block]
        out[layer, block] = mine
        out[1 - layer, block] = other


def contract(sums, t_tiles, spots, place, shares, pair):
    blocks = spots.shape[0]
    ij = t_tiles.shape[1] // 2
    sources = tuple(source for source, _ in shares)
    depth = len(shares) * pair * LANES
    given = [place, spots, t_tiles, *(share for _, share in shares)]
    specs = [SMEM, SMEM] + [VMEM] * (1 + len(shares))
    if sums is not None:
        given.append(sums)
        specs.append(VMEM)

    def kernel(*refs):
        contract_kernel(sources, sums is None, pair, *refs)

    return pl.pallas_call(
        kernel,
        out_shape=jax.ShapeDtypeStruct((2, blocks, ij, LANES), jnp.float32),
        in_specs=specs,
        out_specs=VMEM,
        scratch_shapes=[
            pltpu.VMEM((2, 2 * ij, depth), jnp.bfloat16),
            pltpu.VMEM((2, depth, 2 * LANES), jnp.bfloat16),
        ],
        input_output_aliases={} if sums is None else {len(given) - 1: 0},
        compiler_params=pltpu.CompilerParams(vmem_limit_bytes=32 * 2**20),
        cost_estimate=pl.CostEstimate(
            flops=2 * blocks * 2 * ij * depth * 2 * LANES,
            bytes_accessed=(len(shares) + 4) * 2**19,
            transcendentals=0,
        ),
    )(*given)


def on_device(t_amps, v_tiles, v_where):
    cols = lax.axis_size("col")
    blocks = lax.axis_size("row")
    held, slots = v_tiles.shape[0], v_tiles.shape[3]
    pair = slots // cols
    rows = pair * HALF
    place = jnp.stack([lax.axis_index("col"), lax.axis_index("layer")])

    parts = pack(v_tiles, v_where, cols)
    parts = lax.all_to_all(parts, "col", 0, 0, tiled=True)
    parts = parts.reshape(held * cols, rows + 8, LANES)
    parts = lax.all_to_all(parts, "row", 0, 0, tiled=True)
    spots = parts[:, rows, :slots].astype(jnp.int32)
    own = parts[:, :rows].reshape(blocks * rows, LANES)

    def send(share, to):
        return lax.ppermute(share, "col", [(i, to(i)) for i in range(cols)])

    def up(i):
        return (i + 2) % cols

    def down(i):
        return (i - 2) % cols

    def across(i):
        return i ^ 1

    t_tiles = prepare(t_amps)

    def add(sums, *shares):
        return contract(sums, t_tiles, spots, place, shares, pair)

    half, middle = blocks * rows // 2, blocks // 2
    partner = send(own, across)
    below = send(own, up)
    above = send(own, down)
    sums = add(None, ((0, 0, 0), own))
    sums, partner, below, above = lax.optimization_barrier((sums, partner, below, above))
    partner_below = send(partner, up)
    partner_above = send(partner, down)
    far_low = send(below[:half], up)
    far_high = send(above[half:], down)
    sums = add(sums, ((0, 0, 1), partner), ((0, -2, 0), below), ((0, 2, 0), above))
    sums, far_low, far_high = lax.optimization_barrier((sums, far_low, far_high))
    partner_far_low = send(far_low, across)
    partner_far_high = send(far_high, across)
    sums = add(sums, ((0, 4, 0), far_low), ((middle, 4, 0), far_high))
    sums = add(sums, ((0, -2, 1), partner_below), ((0, 2, 1), partner_above))
    sums = add(sums, ((0, 4, 1), partner_far_low), ((middle, 4, 1), partner_far_high))
    sums = sums[0] + lax.ppermute(sums[1], "layer", [(0, 1), (1, 0)])
    sums = lax.all_to_all(sums, "row", 0, 0, tiled=True)
    return jnp.sum(sums, axis=0)


def solution(mesh):
    return jax.shard_map(
        on_device,
        mesh=mesh,
        in_specs=(
            P("col", ("row", "layer")),
            P("col", "layer", "row", None, None),
            P("col", "layer", "row", None),
        ),
        out_specs=P("col", ("row", "layer")),
        check_vma=False,
    )
```

```python
import jax
import jax.numpy as jnp
from jax import lax
from jax.experimental import pallas as pl
from jax.experimental.pallas import tpu as pltpu
from jax.sharding import PartitionSpec as P

TILE = 64
AB_DEV = 128
LANES = 128
GROUP = 4
HALF = TILE // 2
VMEM = pl.BlockSpec(memory_space=pltpu.VMEM)
SMEM = pl.BlockSpec(memory_space=pltpu.SMEM)


def split_rows(x):
    hi = x.astype(jnp.bfloat16)
    return hi, (x - hi.astype(jnp.float32)).astype(jnp.bfloat16)


def pack_kernel(spots, lists, out):
    held, slots = spots.shape
    cols = out.shape[0]
    pair = slots // cols
    rows = pair * HALF
    lane = lax.broadcasted_iota(jnp.int32, (8, LANES), 1)
    for b in range(held):
        row = jnp.zeros((8, LANES), jnp.float32)
        for s in range(slots):
            row = jnp.where(lane == s, spots[b, s].astype(jnp.float32), row)
        base = b * (rows + 8)
        for c in range(cols):
            for p in range(pair):
                s = c * pair + p
                out[c, base + p * HALF : base + (p + 1) * HALF] = lists[b, s // 8, pl.ds(s % 8, HALF, stride=8), :]
            out[c, base + rows : base + rows + 8] = row


def pack(v_tiles, v_where, cols):
    held, slots = v_tiles.shape[0], v_tiles.shape[3]
    lists = v_tiles.reshape(held, slots // 8, 8, HALF, LANES).transpose(0, 1, 3, 2, 4)
    lists = lists.reshape(held, slots // 8, HALF * 8, LANES)
    return pl.pallas_call(
        pack_kernel,
        out_shape=jax.ShapeDtypeStruct((cols, held * (slots // cols * HALF + 8), LANES), jnp.float32),
        in_specs=[SMEM, VMEM],
        out_specs=VMEM,
        compiler_params=pltpu.CompilerParams(vmem_limit_bytes=16 * 2**20),
        cost_estimate=pl.CostEstimate(flops=0, bytes_accessed=2**20, transcendentals=0),
    )(v_where.reshape(held, slots), lists)


def prepare_kernel(t_ref, t_tiles):
    row = lax.broadcasted_iota(jnp.int32, (LANES, 2 * LANES), 0)
    col = lax.broadcasted_iota(jnp.int32, (LANES, 2 * LANES), 1)
    source = (col // LANES) * TILE + 2 * (col % HALF) + (col % TILE) // HALF
    pick = (row == source).astype(jnp.bfloat16)
    for at in range(t_ref.shape[1] // LANES):
        hi, lo = split_rows(t_ref[:, at * LANES : (at + 1) * LANES])
        both = jnp.dot(
            jnp.concatenate([hi, lo], axis=0), pick, preferred_element_type=jnp.float32
        ).astype(jnp.bfloat16)
        t_tiles[2 * at] = both[:, :LANES]
        t_tiles[2 * at + 1] = both[:, LANES:]


def prepare(t_block):
    ij, cd = t_block.shape
    return pl.pallas_call(
        prepare_kernel,
        out_shape=jax.ShapeDtypeStruct((cd // TILE, 2 * ij, LANES), jnp.bfloat16),
        in_specs=[VMEM],
        out_specs=VMEM,
        compiler_params=pltpu.CompilerParams(vmem_limit_bytes=32 * 2**20),
        cost_estimate=pl.CostEstimate(flops=2 * 2 * ij * cd * 2 * LANES, bytes_accessed=3 * 2**20, transcendentals=0),
    )(t_block)


def slot_rows(v, spot):
    lane_half = lax.broadcasted_iota(jnp.int32, (HALF, LANES), 1) // TILE
    safe = jnp.maximum(spot, 0)
    ab_half = safe & 1
    ab_pair = (safe >> 1) & 1
    swapped = pltpu.roll(v, TILE, 1)
    upper = ab_half == 1
    keep = (lane_half == ab_half) & (spot >= 0)
    hi_e, lo_e = split_rows(jnp.where(keep, jnp.where(upper, swapped, v), 0.0))
    hi_o, lo_o = split_rows(jnp.where(keep, jnp.where(upper, v, swapped), 0.0))
    rows = jnp.concatenate([hi_e, hi_o, lo_e, lo_o], axis=0)
    none = jnp.zeros_like(rows)
    return jnp.where(ab_pair == 0, rows, none), jnp.where(ab_pair == 1, rows, none)


def contract_kernel(sources, offsets, fresh, pair, group, *refs):
    count, blocks_held = len(sources), len(offsets)
    place, spots = refs[:2]
    t_tiles = refs[2 : 2 + blocks_held]
    shares = refs[2 + blocks_held : 2 + blocks_held + count]
    rest = refs[2 + blocks_held + count :]
    sums = None if fresh else rest[0]
    out, lhs, rhs = rest[-3:]
    layer = place[1]
    blocks, ij = out.shape[1:3]
    rows = pair * HALF
    cols = spots.shape[1] // pair
    columns = [((place[0] + shift) & (cols - 1)) ^ flip for _, shift, flip in sources]
    members = [place[2] ^ offset for offset in offsets]
    for block in range(blocks):
        used = [
            n for n in range(count)
            if sources[n][0] <= block < sources[n][0] + shares[n].shape[0] // (group * rows)
        ]
        buffer = block % 2
        at = 0
        for n in used:
            for held in range(blocks_held):
                first = pl.multiple_of(((block - sources[n][0]) * group + members[held]) * rows, rows)
                for p in range(pair):
                    spot = spots[block * group + members[held], columns[n] * pair + p]
                    lhs[buffer, :, at : at + LANES] = t_tiles[held][jnp.maximum(spot, 0) >> 2]
                    left, right = slot_rows(shares[n][pl.ds(first + p * HALF, HALF), :], spot)
                    rhs[buffer, at : at + LANES, :LANES] = left
                    rhs[buffer, at : at + LANES, LANES:] = right
                    at += LANES
        total = jnp.dot(lhs[buffer, :, :at], rhs[buffer, :at], preferred_element_type=jnp.float32)
        total = total[:ij] + total[ij:]
        mine = total[:, :LANES]
        other = total[:, LANES:]
        if sums is not None:
            mine = mine + sums[layer, block]
            other = other + sums[1 - layer, block]
        out[layer, block] = mine
        out[1 - layer, block] = other


def contract(sums, place, spots, held, shares, pair):
    group = GROUP
    blocks = spots.shape[0] // group
    ij = next(iter(held.values())).shape[1] // 2
    sources = tuple(source for source, _ in shares)
    offsets = tuple(held)
    depth = len(shares) * len(held) * pair * LANES
    given = [place, spots, *held.values(), *(share for _, share in shares)]
    specs = [SMEM, SMEM] + [VMEM] * (len(given) - 2)
    if sums is not None:
        given.append(sums)
        specs.append(VMEM)

    def kernel(*refs):
        contract_kernel(sources, offsets, sums is None, pair, group, *refs)

    return pl.pallas_call(
        kernel,
        out_shape=jax.ShapeDtypeStruct((2, blocks, ij, LANES), jnp.float32),
        in_specs=specs,
        out_specs=VMEM,
        scratch_shapes=[
            pltpu.VMEM((2, 2 * ij, depth), jnp.bfloat16),
            pltpu.VMEM((2, depth, 2 * LANES), jnp.bfloat16),
        ],
        input_output_aliases={} if sums is None else {len(given) - 1: 0},
        compiler_params=pltpu.CompilerParams(vmem_limit_bytes=40 * 2**20),
        cost_estimate=pl.CostEstimate(
            flops=2 * blocks * 2 * ij * depth * 2 * LANES,
            bytes_accessed=(len(shares) + 4) * 2**19,
            transcendentals=0,
        ),
    )(*given)


def on_device(t_amps, v_tiles, v_where):
    cols = lax.axis_size("col")
    rows_axis = lax.axis_size("row")
    held, slots = v_tiles.shape[0], v_tiles.shape[3]
    pair = slots // cols
    rows = pair * HALF
    blocks = rows_axis // GROUP
    across_m = [[GROUP * m + member for m in range(blocks)] for member in range(GROUP)]
    place = jnp.stack([lax.axis_index("col"), lax.axis_index("layer"), lax.axis_index("row") % GROUP])

    def send(share, to, axis="col", size=cols):
        return lax.ppermute(share, axis, [(i, to(i)) for i in range(size)])

    def send_t(t_block, offset):
        return send(t_block, lambda i: i ^ offset, "row", rows_axis)

    t_two = send_t(t_amps, 2)
    t_one = send_t(t_amps, 1)

    parts = pack(v_tiles, v_where, cols)
    parts = lax.all_to_all(parts, "col", 0, 0, tiled=True)
    parts = parts.reshape(blocks, GROUP * (rows + 8), LANES)
    parts = lax.all_to_all(parts, "row", 0, 0, tiled=True, axis_index_groups=across_m)
    parts = parts.reshape(blocks * GROUP, rows + 8, LANES)
    spots = parts[:, rows, :slots].astype(jnp.int32)
    own = parts[:, :rows].reshape(blocks * GROUP * rows, LANES)

    def up(i):
        return (i + 2) % cols

    def down(i):
        return (i - 2) % cols

    def across(i):
        return i ^ 1

    def add(sums, held, *shares):
        return contract(sums, place, spots, held, shares, pair)

    half, middle = own.shape[0] // 2, blocks // 2
    partner = send(own, across)
    below = send(own, up)
    above = send(own, down)
    tiles = {0: prepare(t_amps), 2: prepare(t_two)}
    sums = add(None, tiles, ((0, 0, 0), own))
    t_three = send_t(t_one, 2)
    far_low = send(below[:half], up)
    far_high = send(above[half:], down)
    partner_below = send(partner, up)
    partner_above = send(partner, down)
    sums = add(sums, tiles, ((0, 0, 1), partner), ((0, -2, 0), below), ((0, 2, 0), above))
    partner_far_low = send(far_low, across)
    partner_far_high = send(far_high, across)
    one = {1: prepare(t_one)}
    here = [((0, 0, 0), own), ((0, 0, 1), partner), ((0, -2, 0), below), ((0, 2, 0), above)]
    far = [((0, 4, 0), far_low), ((middle, 4, 0), far_high)]
    beside = [((0, -2, 1), partner_below), ((0, 2, 1), partner_above)]
    last = [((0, 4, 1), partner_far_low), ((middle, 4, 1), partner_far_high)]
    sums = add(sums, one, *here)
    three = {**tiles, **one}
    sums = add(sums, three, *far)
    sums = add(sums, three, *beside)
    sums = add(sums, three, *last)
    sums = add(sums, {3: prepare(t_three)}, *here, *far, *beside, *last)

    sums = sums[0] + lax.ppermute(sums[1], "layer", [(0, 1), (1, 0)])
    sums = lax.all_to_all(sums, "row", 0, 0, tiled=True, axis_index_groups=across_m)
    return jnp.sum(sums, axis=0)


def solution(mesh):
    return jax.shard_map(
        on_device,
        mesh=mesh,
        in_specs=(
            P("col", ("row", "layer")),
            P("col", "layer", "row", None, None),
            P("col", "layer", "row", None),
        ),
        out_specs=P("col", ("row", "layer")),
        check_vma=False,
    )
```

```python
import jax
import jax.numpy as jnp
from jax import lax
from jax.experimental import pallas as pl
from jax.experimental.pallas import tpu as pltpu
from jax.sharding import PartitionSpec as P

TILE = 64
AB_DEV = 128
LANES = 128
GROUP = 2
HALF = TILE // 2
VMEM = pl.BlockSpec(memory_space=pltpu.VMEM)
SMEM = pl.BlockSpec(memory_space=pltpu.SMEM)


def split_rows(x):
    hi = x.astype(jnp.bfloat16)
    return hi, (x - hi.astype(jnp.float32)).astype(jnp.bfloat16)


def pack_kernel(spots, lists, out):
    held, slots = spots.shape
    cols = out.shape[0]
    pair = slots // cols
    rows = pair * HALF
    lane = lax.broadcasted_iota(jnp.int32, (8, LANES), 1)
    for b in range(held):
        row = jnp.zeros((8, LANES), jnp.float32)
        for s in range(slots):
            row = jnp.where(lane == s, spots[b, s].astype(jnp.float32), row)
        base = b * (rows + 8)
        for c in range(cols):
            for p in range(pair):
                s = c * pair + p
                out[c, base + p * HALF : base + (p + 1) * HALF] = lists[b, s // 8, pl.ds(s % 8, HALF, stride=8), :]
            out[c, base + rows : base + rows + 8] = row


def pack(v_tiles, v_where, cols):
    held, slots = v_tiles.shape[0], v_tiles.shape[3]
    lists = v_tiles.reshape(held, slots // 8, 8, HALF, LANES).transpose(0, 1, 3, 2, 4)
    lists = lists.reshape(held, slots // 8, HALF * 8, LANES)
    return pl.pallas_call(
        pack_kernel,
        out_shape=jax.ShapeDtypeStruct((cols, held * (slots // cols * HALF + 8), LANES), jnp.float32),
        in_specs=[SMEM, VMEM],
        out_specs=VMEM,
        compiler_params=pltpu.CompilerParams(vmem_limit_bytes=16 * 2**20),
        cost_estimate=pl.CostEstimate(flops=0, bytes_accessed=2**20, transcendentals=0),
    )(v_where.reshape(held, slots), lists)


def prepare_kernel(t_ref, t_tiles):
    row = lax.broadcasted_iota(jnp.int32, (LANES, 2 * LANES), 0)
    col = lax.broadcasted_iota(jnp.int32, (LANES, 2 * LANES), 1)
    source = (col // LANES) * TILE + 2 * (col % HALF) + (col % TILE) // HALF
    pick = (row == source).astype(jnp.bfloat16)
    for at in range(t_ref.shape[1] // LANES):
        hi, lo = split_rows(t_ref[:, at * LANES : (at + 1) * LANES])
        both = jnp.dot(
            jnp.concatenate([hi, lo], axis=0), pick, preferred_element_type=jnp.float32
        ).astype(jnp.bfloat16)
        t_tiles[2 * at] = both[:, :LANES]
        t_tiles[2 * at + 1] = both[:, LANES:]


def prepare(t_block):
    ij, cd = t_block.shape
    return pl.pallas_call(
        prepare_kernel,
        out_shape=jax.ShapeDtypeStruct((cd // TILE, 2 * ij, LANES), jnp.bfloat16),
        in_specs=[VMEM],
        out_specs=VMEM,
        compiler_params=pltpu.CompilerParams(vmem_limit_bytes=32 * 2**20),
        cost_estimate=pl.CostEstimate(flops=2 * 2 * ij * cd * 2 * LANES, bytes_accessed=3 * 2**20, transcendentals=0),
    )(t_block)


def slot_rows(v, spot):
    lane_half = lax.broadcasted_iota(jnp.int32, (HALF, LANES), 1) // TILE
    safe = jnp.maximum(spot, 0)
    ab_half = safe & 1
    ab_pair = (safe >> 1) & 1
    swapped = pltpu.roll(v, TILE, 1)
    upper = ab_half == 1
    keep = (lane_half == ab_half) & (spot >= 0)
    hi_e, lo_e = split_rows(jnp.where(keep, jnp.where(upper, swapped, v), 0.0))
    hi_o, lo_o = split_rows(jnp.where(keep, jnp.where(upper, v, swapped), 0.0))
    rows = jnp.concatenate([hi_e, hi_o, lo_e, lo_o], axis=0)
    none = jnp.zeros_like(rows)
    return jnp.where(ab_pair == 0, rows, none), jnp.where(ab_pair == 1, rows, none)


def contract_kernel(sources, offsets, fresh, pair, group, *refs):
    count, blocks_held = len(sources), len(offsets)
    place, spots = refs[:2]
    t_tiles = refs[2 : 2 + blocks_held]
    shares = refs[2 + blocks_held : 2 + blocks_held + count]
    rest = refs[2 + blocks_held + count :]
    sums = None if fresh else rest[0]
    out, lhs, rhs = rest[-3:]
    layer = place[1]
    blocks, ij = out.shape[1:3]
    rows = pair * HALF
    cols = spots.shape[1] // pair
    columns = [((place[0] + shift) & (cols - 1)) ^ flip for _, shift, flip in sources]
    members = [place[2] ^ offset for offset in offsets]
    for block in range(blocks):
        used = [
            n for n in range(count)
            if sources[n][0] <= block < sources[n][0] + shares[n].shape[0] // (group * rows)
        ]
        buffer = block % 2
        at = 0
        for n in used:
            for held in range(blocks_held):
                first = pl.multiple_of(((block - sources[n][0]) * group + members[held]) * rows, rows)
                for p in range(pair):
                    spot = spots[block * group + members[held], columns[n] * pair + p]
                    lhs[buffer, :, at : at + LANES] = t_tiles[held][jnp.maximum(spot, 0) >> 2]
                    left, right = slot_rows(shares[n][pl.ds(first + p * HALF, HALF), :], spot)
                    rhs[buffer, at : at + LANES, :LANES] = left
                    rhs[buffer, at : at + LANES, LANES:] = right
                    at += LANES
        total = jnp.dot(lhs[buffer, :, :at], rhs[buffer, :at], preferred_element_type=jnp.float32)
        total = total[:ij] + total[ij:]
        mine = total[:, :LANES]
        other = total[:, LANES:]
        if sums is not None:
            mine = mine + sums[layer, block]
            other = other + sums[1 - layer, block]
        out[layer, block] = mine
        out[1 - layer, block] = other


def contract(sums, place, spots, held, shares, pair):
    group = GROUP
    blocks = spots.shape[0] // group
    ij = next(iter(held.values())).shape[1] // 2
    sources = tuple(source for source, _ in shares)
    offsets = tuple(held)
    depth = len(shares) * len(held) * pair * LANES
    given = [place, spots, *held.values(), *(share for _, share in shares)]
    specs = [SMEM, SMEM] + [VMEM] * (len(given) - 2)
    if sums is not None:
        given.append(sums)
        specs.append(VMEM)

    def kernel(*refs):
        contract_kernel(sources, offsets, sums is None, pair, group, *refs)

    return pl.pallas_call(
        kernel,
        out_shape=jax.ShapeDtypeStruct((2, blocks, ij, LANES), jnp.float32),
        in_specs=specs,
        out_specs=VMEM,
        scratch_shapes=[
            pltpu.VMEM((2, 2 * ij, depth), jnp.bfloat16),
            pltpu.VMEM((2, depth, 2 * LANES), jnp.bfloat16),
        ],
        input_output_aliases={} if sums is None else {len(given) - 1: 0},
        compiler_params=pltpu.CompilerParams(vmem_limit_bytes=40 * 2**20),
        cost_estimate=pl.CostEstimate(
            flops=2 * blocks * 2 * ij * depth * 2 * LANES,
            bytes_accessed=(len(shares) + 4) * 2**19,
            transcendentals=0,
        ),
    )(*given)


def on_device(t_amps, v_tiles, v_where):
    cols = lax.axis_size("col")
    rows_axis = lax.axis_size("row")
    held, slots = v_tiles.shape[0], v_tiles.shape[3]
    pair = slots // cols
    rows = pair * HALF
    blocks = rows_axis // GROUP
    across_m = [[GROUP * m + member for m in range(blocks)] for member in range(GROUP)]
    place = jnp.stack([lax.axis_index("col"), lax.axis_index("layer"), lax.axis_index("row") % GROUP])

    def send(share, to, axis="col", size=cols):
        return lax.ppermute(share, axis, [(i, to(i)) for i in range(size)])

    def send_t(t_block, offset):
        return send(t_block, lambda i: i ^ offset, "row", rows_axis)

    t_other = send_t(t_amps, 1)

    parts = pack(v_tiles, v_where, cols)
    parts = lax.all_to_all(parts, "col", 0, 0, tiled=True)
    parts = parts.reshape(blocks, GROUP * (rows + 8), LANES)
    parts = lax.all_to_all(parts, "row", 0, 0, tiled=True, axis_index_groups=across_m)
    parts = parts.reshape(blocks * GROUP, rows + 8, LANES)
    spots = parts[:, rows, :slots].astype(jnp.int32)
    own = parts[:, :rows].reshape(blocks * GROUP * rows, LANES)

    def up(i):
        return (i + 2) % cols

    def down(i):
        return (i - 2) % cols

    def across(i):
        return i ^ 1

    def add(sums, held, *shares):
        return contract(sums, place, spots, held, shares, pair)

    half, middle = own.shape[0] // 2, blocks // 2
    partner = send(own, across)
    below = send(own, up)
    above = send(own, down)
    tiles = {0: prepare(t_amps)}
    sums = add(None, tiles, ((0, 0, 0), own))
    sums, partner = lax.optimization_barrier((sums, partner))
    far_low = send(below[:half], up)
    far_high = send(above[half:], down)
    partner_below = send(partner, up)
    partner_above = send(partner, down)
    other = {1: prepare(t_other)}
    both = {**tiles, **other}
    sums = add(sums, both, ((0, 0, 1), partner), ((0, -2, 0), below), ((0, 2, 0), above))
    sums, far_low, far_high = lax.optimization_barrier((sums, far_low, far_high))
    partner_far_low = send(far_low, across)
    partner_far_high = send(far_high, across)
    sums = add(sums, other, ((0, 0, 0), own))
    sums = add(sums, both, ((0, 4, 0), far_low), ((middle, 4, 0), far_high))
    sums = add(sums, both, ((0, -2, 1), partner_below), ((0, 2, 1), partner_above))
    sums = add(sums, both, ((0, 4, 1), partner_far_low), ((middle, 4, 1), partner_far_high))

    sums = sums[0] + lax.ppermute(sums[1], "layer", [(0, 1), (1, 0)])
    sums = lax.all_to_all(sums, "row", 0, 0, tiled=True, axis_index_groups=across_m)
    return jnp.sum(sums, axis=0)


def solution(mesh):
    return jax.shard_map(
        on_device,
        mesh=mesh,
        in_specs=(
            P("col", ("row", "layer")),
            P("col", "layer", "row", None, None),
            P("col", "layer", "row", None),
        ),
        out_specs=P("col", ("row", "layer")),
        check_vma=False,
    )
```

```python
import jax
import jax.numpy as jnp
from jax import lax
from jax.experimental import pallas as pl
from jax.experimental.pallas import tpu as pltpu
from jax.sharding import PartitionSpec as P

TILE = 64
AB_DEV = 128
LANES = 128
GROUP = 2
HALF = TILE // 2
VMEM = pl.BlockSpec(memory_space=pltpu.VMEM)
SMEM = pl.BlockSpec(memory_space=pltpu.SMEM)


def split_rows(x):
    hi = x.astype(jnp.bfloat16)
    return hi, (x - hi.astype(jnp.float32)).astype(jnp.bfloat16)


def pack_kernel(spots, lists, out):
    held, slots = spots.shape
    cols = out.shape[0]
    pair = slots // cols
    rows = pair * HALF
    lane = lax.broadcasted_iota(jnp.int32, (8, LANES), 1)
    for b in range(held):
        row = jnp.zeros((8, LANES), jnp.float32)
        for s in range(slots):
            row = jnp.where(lane == s, spots[b, s].astype(jnp.float32), row)
        base = b * (rows + 8)
        for c in range(cols):
            for p in range(pair):
                s = c * pair + p
                out[c, base + p * HALF : base + (p + 1) * HALF] = lists[b, s // 8, pl.ds(s % 8, HALF, stride=8), :]
            out[c, base + rows : base + rows + 8] = row


def pack(v_tiles, v_where, cols):
    held, slots = v_tiles.shape[0], v_tiles.shape[3]
    lists = v_tiles.reshape(held, slots // 8, 8, HALF, LANES).transpose(0, 1, 3, 2, 4)
    lists = lists.reshape(held, slots // 8, HALF * 8, LANES)
    return pl.pallas_call(
        pack_kernel,
        out_shape=jax.ShapeDtypeStruct((cols, held * (slots // cols * HALF + 8), LANES), jnp.float32),
        in_specs=[SMEM, VMEM],
        out_specs=VMEM,
        compiler_params=pltpu.CompilerParams(vmem_limit_bytes=14 * 2**20),
        cost_estimate=pl.CostEstimate(flops=0, bytes_accessed=2**20, transcendentals=0),
    )(v_where.reshape(held, slots), lists)


def prepare_kernel(*refs):
    *halves, t_tiles = refs
    row = lax.broadcasted_iota(jnp.int32, (LANES, 2 * LANES), 0)
    col = lax.broadcasted_iota(jnp.int32, (LANES, 2 * LANES), 1)
    source = (col // LANES) * TILE + 2 * (col % HALF) + (col % TILE) // HALF
    pick = (row == source).astype(jnp.bfloat16)
    for at in range(halves[0].shape[1] // LANES):
        split = [split_rows(half[:, at * LANES : (at + 1) * LANES]) for half in halves]
        rows = jnp.concatenate([hi for hi, _ in split] + [lo for _, lo in split], axis=0)
        both = jnp.dot(rows, pick, preferred_element_type=jnp.float32).astype(jnp.bfloat16)
        t_tiles[2 * at] = both[:, :LANES]
        t_tiles[2 * at + 1] = both[:, LANES:]


def prepare(*halves):
    ij, cd = sum(half.shape[0] for half in halves), halves[0].shape[1]
    return pl.pallas_call(
        prepare_kernel,
        out_shape=jax.ShapeDtypeStruct((cd // TILE, 2 * ij, LANES), jnp.bfloat16),
        in_specs=[VMEM] * len(halves),
        out_specs=VMEM,
        compiler_params=pltpu.CompilerParams(vmem_limit_bytes=14 * 2**20),
        cost_estimate=pl.CostEstimate(flops=2 * 2 * ij * cd * 2 * LANES, bytes_accessed=3 * 2**20, transcendentals=0),
    )(*halves)


def slot_rows(v, spot):
    lane_half = lax.broadcasted_iota(jnp.int32, (HALF, LANES), 1) // TILE
    safe = jnp.maximum(spot, 0)
    ab_half = safe & 1
    ab_pair = (safe >> 1) & 1
    swapped = pltpu.roll(v, TILE, 1)
    upper = ab_half == 1
    keep = (lane_half == ab_half) & (spot >= 0)
    hi_e, lo_e = split_rows(jnp.where(keep, jnp.where(upper, swapped, v), 0.0))
    hi_o, lo_o = split_rows(jnp.where(keep, jnp.where(upper, v, swapped), 0.0))
    rows = jnp.concatenate([hi_e, hi_o, lo_e, lo_o], axis=0)
    none = jnp.zeros_like(rows)
    return jnp.where(ab_pair == 0, rows, none), jnp.where(ab_pair == 1, rows, none)


def contract_kernel(sources, offsets, fresh, pair, group, *refs):
    count, blocks_held = len(sources), len(offsets)
    place, spots = refs[:2]
    t_tiles = refs[2 : 2 + blocks_held]
    shares = refs[2 + blocks_held : 2 + blocks_held + count]
    rest = refs[2 + blocks_held + count :]
    sums = None if fresh else rest[0]
    out, lhs, rhs = rest[-3:]
    layer = place[1]
    blocks, ij = out.shape[1:3]
    rows = pair * HALF
    cols = spots.shape[1] // pair
    columns = [((place[0] + shift) & (cols - 1)) ^ flip for _, shift, flip in sources]
    members = [place[2] ^ offset for offset in offsets]
    for block in range(blocks):
        used = [
            n for n in range(count)
            if sources[n][0] <= block < sources[n][0] + shares[n].shape[0] // (group * rows)
        ]
        buffer = block % 2
        at = 0
        for n in used:
            for held in range(blocks_held):
                first = pl.multiple_of(((block - sources[n][0]) * group + members[held]) * rows, rows)
                for p in range(pair):
                    spot = spots[block * group + members[held], columns[n] * pair + p]
                    lhs[buffer, :, at : at + LANES] = t_tiles[held][jnp.maximum(spot, 0) >> 2]
                    left, right = slot_rows(shares[n][pl.ds(first + p * HALF, HALF), :], spot)
                    rhs[buffer, at : at + LANES, :LANES] = left
                    rhs[buffer, at : at + LANES, LANES:] = right
                    at += LANES
        total = jnp.dot(lhs[buffer, :, :at], rhs[buffer, :at], preferred_element_type=jnp.float32)
        total = total[:ij] + total[ij:]
        mine = total[:, :LANES]
        other = total[:, LANES:]
        if sums is not None:
            mine = mine + sums[layer, block]
            other = other + sums[1 - layer, block]
        out[layer, block] = mine
        out[1 - layer, block] = other


def contract(sums, place, spots, held, shares, pair):
    group = GROUP
    blocks = spots.shape[0] // group
    ij = next(iter(held.values())).shape[1] // 2
    sources = tuple(source for source, _ in shares)
    offsets = tuple(held)
    depth = len(shares) * len(held) * pair * LANES
    given = [place, spots, *held.values(), *(share for _, share in shares)]
    specs = [SMEM, SMEM] + [VMEM] * (len(given) - 2)
    if sums is not None:
        given.append(sums)
        specs.append(VMEM)

    def kernel(*refs):
        contract_kernel(sources, offsets, sums is None, pair, group, *refs)

    return pl.pallas_call(
        kernel,
        out_shape=jax.ShapeDtypeStruct((2, blocks, ij, LANES), jnp.float32),
        in_specs=specs,
        out_specs=VMEM,
        scratch_shapes=[
            pltpu.VMEM((2, 2 * ij, depth), jnp.bfloat16),
            pltpu.VMEM((2, depth, 2 * LANES), jnp.bfloat16),
        ],
        input_output_aliases={} if sums is None else {len(given) - 1: 0},
        compiler_params=pltpu.CompilerParams(vmem_limit_bytes=14 * 2**20),
        cost_estimate=pl.CostEstimate(
            flops=2 * blocks * 2 * ij * depth * 2 * LANES,
            bytes_accessed=(len(shares) + 4) * 2**19,
            transcendentals=0,
        ),
    )(*given)


def on_device(t_amps, v_tiles, v_where):
    cols = lax.axis_size("col")
    rows_axis = lax.axis_size("row")
    held, slots = v_tiles.shape[0], v_tiles.shape[3]
    pair = slots // cols
    rows = pair * HALF
    blocks = rows_axis // GROUP
    ranks = [[2 * (GROUP * m + member) + x for m in range(blocks // 2) for x in range(2)] for member in range(GROUP)]
    place = jnp.stack([lax.axis_index("col"), lax.axis_index("layer"), lax.axis_index("row") // 2 % GROUP])

    def send(share, to, axis="col", size=cols):
        return lax.ppermute(share, axis, [(i, to(i)) for i in range(size)])

    def send_t(t_block):
        return send(t_block, lambda i: i ^ 2, "row", rows_axis)

    ij_half = t_amps.shape[0] // 2
    t_first = send_t(t_amps[:ij_half])
    parts = pack(v_tiles, v_where, cols)
    parts = lax.all_to_all(parts, "col", 0, 0, tiled=True)
    parts, t_first = lax.optimization_barrier((parts, t_first))
    parts = parts.reshape(blocks // 2, GROUP, 2, rows + 8, LANES).transpose(0, 2, 1, 3, 4)
    parts = parts.reshape(blocks, GROUP * (rows + 8), LANES)
    parts = lax.all_to_all(parts, "row", 0, 0, tiled=True, axis_index_groups=ranks)
    parts = parts.reshape(blocks * GROUP, rows + 8, LANES)
    spots = parts[:, rows, :slots].astype(jnp.int32)
    own = parts[:, :rows].reshape(blocks * GROUP * rows, LANES)
    own, t_rest = lax.optimization_barrier((own, t_amps[ij_half:]))

    def up(i):
        return (i + 2) % cols

    def down(i):
        return (i - 2) % cols

    def across(i):
        return i ^ 1

    def add(sums, held, *shares):
        return contract(sums, place, spots, held, shares, pair)

    half, middle = own.shape[0] // 2, blocks // 2
    partner = send(own, across)
    below = send(own, up)
    above = send(own, down)
    t_rest = send_t(t_rest)
    tiles = {0: prepare(t_amps)}
    far_low = send(below[:half], up)
    far_high = send(above[half:], down)
    partner_below = send(partner, up)
    partner_above = send(partner, down)
    partner_far_low = send(far_low, across)
    partner_far_high = send(far_high, across)
    near = [((0, 0, 0), own), ((0, 0, 1), partner), ((0, -2, 0), below), ((0, 2, 0), above)]
    sums = add(None, tiles, *near)
    other = {1: prepare(t_first, t_rest)}
    sums = add(sums, other, *near)
    both = {**tiles, **other}
    sums = add(sums, both, ((0, 4, 0), far_low), ((middle, 4, 0), far_high))
    sums = add(sums, both, ((0, -2, 1), partner_below), ((0, 2, 1), partner_above))
    sums = add(sums, both, ((0, 4, 1), partner_far_low), ((middle, 4, 1), partner_far_high))

    sums = sums[0] + lax.ppermute(sums[1], "layer", [(0, 1), (1, 0)])
    sums = lax.all_to_all(sums, "row", 0, 0, tiled=True, axis_index_groups=ranks)
    return jnp.sum(sums, axis=0)


def solution(mesh):
    return jax.shard_map(
        on_device,
        mesh=mesh,
        in_specs=(
            P("col", ("row", "layer")),
            P("col", "layer", "row", None, None),
            P("col", "layer", "row", None),
        ),
        out_specs=P("col", ("row", "layer")),
        check_vma=False,
    )
```

```python
import jax
import jax.numpy as jnp
from jax import lax
from jax.experimental import pallas as pl
from jax.experimental.pallas import tpu as pltpu
from jax.sharding import PartitionSpec as P

TILE = 64
AB_DEV = 128
LANES = 128
GROUP = 2
HALF = TILE // 2
VMEM = pl.BlockSpec(memory_space=pltpu.VMEM)
SMEM = pl.BlockSpec(memory_space=pltpu.SMEM)


def split_rows(x):
    hi = x.astype(jnp.bfloat16)
    return hi, (x - hi.astype(jnp.float32)).astype(jnp.bfloat16)


def pack_kernel(spots, lists, out):
    held, slots = spots.shape
    cols = out.shape[0]
    pair = slots // cols
    rows = pair * HALF
    lane = lax.broadcasted_iota(jnp.int32, (8, LANES), 1)
    for b in range(held):
        row = jnp.zeros((8, LANES), jnp.float32)
        for s in range(slots):
            row = jnp.where(lane == s, spots[b, s].astype(jnp.float32), row)
        base = b * (rows + 8)
        for c in range(cols):
            for p in range(pair):
                s = c * pair + p
                out[c, base + p * HALF : base + (p + 1) * HALF] = lists[b, s // 8, pl.ds(s % 8, HALF, stride=8), :]
            out[c, base + rows : base + rows + 8] = row


def pack(v_tiles, v_where, cols):
    held, slots = v_tiles.shape[0], v_tiles.shape[3]
    lists = v_tiles.reshape(held, slots // 8, 8, HALF, LANES).transpose(0, 1, 3, 2, 4)
    lists = lists.reshape(held, slots // 8, HALF * 8, LANES)
    return pl.pallas_call(
        pack_kernel,
        out_shape=jax.ShapeDtypeStruct((cols, held * (slots // cols * HALF + 8), LANES), jnp.float32),
        in_specs=[SMEM, VMEM],
        out_specs=VMEM,
        compiler_params=pltpu.CompilerParams(vmem_limit_bytes=14 * 2**20),
        cost_estimate=pl.CostEstimate(flops=0, bytes_accessed=2**20, transcendentals=0),
    )(v_where.reshape(held, slots), lists)


def prepare_kernel(*refs):
    *halves, t_tiles = refs
    row = lax.broadcasted_iota(jnp.int32, (LANES, 2 * LANES), 0)
    col = lax.broadcasted_iota(jnp.int32, (LANES, 2 * LANES), 1)
    source = (col // LANES) * TILE + 2 * (col % HALF) + (col % TILE) // HALF
    pick = (row == source).astype(jnp.bfloat16)
    for at in range(halves[0].shape[1] // LANES):
        split = [split_rows(half[:, at * LANES : (at + 1) * LANES]) for half in halves]
        rows = jnp.concatenate([hi for hi, _ in split] + [lo for _, lo in split], axis=0)
        both = jnp.dot(rows, pick, preferred_element_type=jnp.float32).astype(jnp.bfloat16)
        t_tiles[2 * at] = both[:, :LANES]
        t_tiles[2 * at + 1] = both[:, LANES:]


def prepare(*halves):
    ij, cd = sum(half.shape[0] for half in halves), halves[0].shape[1]
    return pl.pallas_call(
        prepare_kernel,
        out_shape=jax.ShapeDtypeStruct((cd // TILE, 2 * ij, LANES), jnp.bfloat16),
        in_specs=[VMEM] * len(halves),
        out_specs=VMEM,
        compiler_params=pltpu.CompilerParams(vmem_limit_bytes=14 * 2**20),
        cost_estimate=pl.CostEstimate(flops=2 * 2 * ij * cd * 2 * LANES, bytes_accessed=3 * 2**20, transcendentals=0),
    )(*halves)


def slot_rows(v, spot):
    lane_half = lax.broadcasted_iota(jnp.int32, (HALF, LANES), 1) // TILE
    safe = jnp.maximum(spot, 0)
    ab_half = safe & 1
    ab_pair = (safe >> 1) & 1
    swapped = pltpu.roll(v, TILE, 1)
    upper = ab_half == 1
    keep = (lane_half == ab_half) & (spot >= 0)
    hi_e, lo_e = split_rows(jnp.where(keep, jnp.where(upper, swapped, v), 0.0))
    hi_o, lo_o = split_rows(jnp.where(keep, jnp.where(upper, v, swapped), 0.0))
    rows = jnp.concatenate([hi_e, hi_o, lo_e, lo_o], axis=0)
    none = jnp.zeros_like(rows)
    return jnp.where(ab_pair == 0, rows, none), jnp.where(ab_pair == 1, rows, none)


def contract_kernel(sources, offsets, fresh, pair, group, *refs):
    count, blocks_held = len(sources), len(offsets)
    place, spots = refs[:2]
    t_tiles = refs[2 : 2 + blocks_held]
    shares = refs[2 + blocks_held : 2 + blocks_held + count]
    rest = refs[2 + blocks_held + count :]
    sums = None if fresh else rest[0]
    out, lhs, rhs = rest[-3:]
    layer = place[1]
    blocks, ij = out.shape[1:3]
    rows = pair * HALF
    cols = spots.shape[1] // pair
    columns = [((place[0] + shift) & (cols - 1)) ^ flip for _, shift, flip in sources]
    members = [place[2] ^ offset for offset in offsets]
    for block in range(blocks):
        used = [
            n for n in range(count)
            if sources[n][0] <= block < sources[n][0] + shares[n].shape[0] // (group * rows)
        ]
        buffer = block % 2
        at = 0
        for n in used:
            for held in range(blocks_held):
                first = pl.multiple_of(((block - sources[n][0]) * group + members[held]) * rows, rows)
                for p in range(pair):
                    spot = spots[block * group + members[held], columns[n] * pair + p]
                    lhs[buffer, :, at : at + LANES] = t_tiles[held][jnp.maximum(spot, 0) >> 2]
                    left, right = slot_rows(shares[n][pl.ds(first + p * HALF, HALF), :], spot)
                    rhs[buffer, at : at + LANES, :LANES] = left
                    rhs[buffer, at : at + LANES, LANES:] = right
                    at += LANES
        total = jnp.dot(lhs[buffer, :, :at], rhs[buffer, :at], preferred_element_type=jnp.float32)
        total = total[:ij] + total[ij:]
        mine = total[:, :LANES]
        other = total[:, LANES:]
        if sums is not None:
            mine = mine + sums[layer, block]
            other = other + sums[1 - layer, block]
        out[layer, block] = mine
        out[1 - layer, block] = other


def contract(sums, place, spots, held, shares, pair):
    group = GROUP
    blocks = spots.shape[0] // group
    ij = next(iter(held.values())).shape[1] // 2
    sources = tuple(source for source, _ in shares)
    offsets = tuple(held)
    depth = len(shares) * len(held) * pair * LANES
    given = [place, spots, *held.values(), *(share for _, share in shares)]
    specs = [SMEM, SMEM] + [VMEM] * (len(given) - 2)
    if sums is not None:
        given.append(sums)
        specs.append(VMEM)

    def kernel(*refs):
        contract_kernel(sources, offsets, sums is None, pair, group, *refs)

    return pl.pallas_call(
        kernel,
        out_shape=jax.ShapeDtypeStruct((2, blocks, ij, LANES), jnp.float32),
        in_specs=specs,
        out_specs=VMEM,
        scratch_shapes=[
            pltpu.VMEM((2, 2 * ij, depth), jnp.bfloat16),
            pltpu.VMEM((2, depth, 2 * LANES), jnp.bfloat16),
        ],
        input_output_aliases={} if sums is None else {len(given) - 1: 0},
        compiler_params=pltpu.CompilerParams(vmem_limit_bytes=14 * 2**20),
        cost_estimate=pl.CostEstimate(
            flops=2 * blocks * 2 * ij * depth * 2 * LANES,
            bytes_accessed=(len(shares) + 4) * 2**19,
            transcendentals=0,
        ),
    )(*given)


def on_device(t_amps, v_tiles, v_where):
    cols = lax.axis_size("col")
    rows_axis = lax.axis_size("row")
    held, slots = v_tiles.shape[0], v_tiles.shape[3]
    pair = slots // cols
    rows = pair * HALF
    blocks = rows_axis // GROUP
    ranks = [
        [2 * (GROUP * m + (m.bit_count() + odd) % 2) + x for m in range(blocks // 2) for x in range(2)]
        for odd in range(2)
    ]
    place = jnp.stack([lax.axis_index("col"), lax.axis_index("layer"), lax.axis_index("row") // 2 % GROUP])

    def send(share, to, axis="col", size=cols):
        return lax.ppermute(share, axis, [(i, to(i)) for i in range(size)])

    def send_t(t_block):
        return send(t_block, lambda i: i ^ 2, "row", rows_axis)

    parts = pack(v_tiles, v_where, cols)
    parts = lax.all_to_all(parts, "col", 0, 0, tiled=True)
    parts = parts.reshape(blocks // 2, GROUP, 2, rows + 8, LANES).transpose(0, 2, 1, 3, 4)
    parts = parts.reshape(blocks, GROUP * (rows + 8), LANES)
    parts = lax.all_to_all(parts, "row", 0, 0, tiled=True, axis_index_groups=ranks)
    parts = parts.reshape(blocks * GROUP, rows + 8, LANES)
    spots = parts[:, rows, :slots].astype(jnp.int32)
    own = parts[:, :rows].reshape(blocks * GROUP * rows, LANES)
    own, t_other = lax.optimization_barrier((own, t_amps))

    def up(i):
        return (i + 2) % cols

    def down(i):
        return (i - 2) % cols

    def across(i):
        return i ^ 1

    def add(sums, held, *shares):
        return contract(sums, place, spots, held, shares, pair)

    half, middle = own.shape[0] // 2, blocks // 2
    partner = send(own, across)
    below = send(own, up)
    above = send(own, down)
    t_other = send_t(t_other)
    tiles = {0: prepare(t_amps)}
    far_low = send(below[:half], up)
    far_high = send(above[half:], down)
    partner_below = send(partner, up)
    partner_above = send(partner, down)
    partner_far_low = send(far_low, across)
    partner_far_high = send(far_high, across)
    near = [((0, 0, 0), own), ((0, 0, 1), partner), ((0, -2, 0), below), ((0, 2, 0), above)]
    sums = add(None, tiles, *near)
    other = {1: prepare(t_other)}
    sums = add(sums, other, *near)
    both = {**tiles, **other}
    sums = add(sums, both, ((0, 4, 0), far_low), ((middle, 4, 0), far_high))
    sums = add(sums, both, ((0, -2, 1), partner_below), ((0, 2, 1), partner_above))
    sums = add(sums, both, ((0, 4, 1), partner_far_low), ((middle, 4, 1), partner_far_high))

    sums = sums[0] + lax.ppermute(sums[1], "layer", [(0, 1), (1, 0)])
    sums = lax.all_to_all(sums, "row", 0, 0, tiled=True, axis_index_groups=ranks)
    return jnp.sum(sums, axis=0)


def solution(mesh):
    return jax.shard_map(
        on_device,
        mesh=mesh,
        in_specs=(
            P("col", ("row", "layer")),
            P("col", "layer", "row", None, None),
            P("col", "layer", "row", None),
        ),
        out_specs=P("col", ("row", "layer")),
        check_vma=False,
    )
```

```python
import jax
import jax.numpy as jnp
from jax import lax
from jax.experimental import pallas as pl
from jax.experimental.pallas import tpu as pltpu
from jax.sharding import PartitionSpec as P

TILE = 64
AB_DEV = 128
LANES = 128
GROUP = 2
HALF = TILE // 2
VMEM = pl.BlockSpec(memory_space=pltpu.VMEM)
SMEM = pl.BlockSpec(memory_space=pltpu.SMEM)


def split_rows(x):
    hi = x.astype(jnp.bfloat16)
    return hi, (x - hi.astype(jnp.float32)).astype(jnp.bfloat16)


def pack_kernel(spots, lists, out):
    held, slots = spots.shape
    cols = out.shape[0]
    pair = slots // cols
    rows = pair * HALF
    lane = lax.broadcasted_iota(jnp.int32, (8, LANES), 1)
    for b in range(held):
        row = jnp.zeros((8, LANES), jnp.float32)
        for s in range(slots):
            row = jnp.where(lane == s, spots[b, s].astype(jnp.float32), row)
        base = b * (rows + 8)
        for c in range(cols):
            for p in range(pair):
                s = c * pair + p
                out[c, base + p * HALF : base + (p + 1) * HALF] = lists[b, s // 8, pl.ds(s % 8, HALF, stride=8), :]
            out[c, base + rows : base + rows + 8] = row


def pack(v_tiles, v_where, cols):
    held, slots = v_tiles.shape[0], v_tiles.shape[3]
    lists = v_tiles.reshape(held, slots // 8, 8, HALF, LANES).transpose(0, 1, 3, 2, 4)
    lists = lists.reshape(held, slots // 8, HALF * 8, LANES)
    return pl.pallas_call(
        pack_kernel,
        out_shape=jax.ShapeDtypeStruct((cols, held * (slots // cols * HALF + 8), LANES), jnp.float32),
        in_specs=[SMEM, VMEM],
        out_specs=VMEM,
        compiler_params=pltpu.CompilerParams(vmem_limit_bytes=14 * 2**20),
        cost_estimate=pl.CostEstimate(flops=0, bytes_accessed=2**20, transcendentals=0),
    )(v_where.reshape(held, slots), lists)


def prepare_kernel(*refs):
    *halves, t_tiles = refs
    row = lax.broadcasted_iota(jnp.int32, (LANES, 2 * LANES), 0)
    col = lax.broadcasted_iota(jnp.int32, (LANES, 2 * LANES), 1)
    source = (col // LANES) * TILE + 2 * (col % HALF) + (col % TILE) // HALF
    pick = (row == source).astype(jnp.bfloat16)
    for at in range(halves[0].shape[1] // LANES):
        split = [split_rows(half[:, at * LANES : (at + 1) * LANES]) for half in halves]
        rows = jnp.concatenate([hi for hi, _ in split] + [lo for _, lo in split], axis=0)
        both = jnp.dot(rows, pick, preferred_element_type=jnp.float32).astype(jnp.bfloat16)
        t_tiles[2 * at] = both[:, :LANES]
        t_tiles[2 * at + 1] = both[:, LANES:]


def prepare(*halves):
    ij, cd = sum(half.shape[0] for half in halves), halves[0].shape[1]
    return pl.pallas_call(
        prepare_kernel,
        out_shape=jax.ShapeDtypeStruct((cd // TILE, 2 * ij, LANES), jnp.bfloat16),
        in_specs=[VMEM] * len(halves),
        out_specs=VMEM,
        compiler_params=pltpu.CompilerParams(vmem_limit_bytes=14 * 2**20),
        cost_estimate=pl.CostEstimate(flops=2 * 2 * ij * cd * 2 * LANES, bytes_accessed=3 * 2**20, transcendentals=0),
    )(*halves)


def slot_rows(v, spot):
    lane_half = lax.broadcasted_iota(jnp.int32, (HALF, LANES), 1) // TILE
    safe = jnp.maximum(spot, 0)
    ab_half = safe & 1
    ab_pair = (safe >> 1) & 1
    swapped = pltpu.roll(v, TILE, 1)
    upper = ab_half == 1
    keep = (lane_half == ab_half) & (spot >= 0)
    hi_e, lo_e = split_rows(jnp.where(keep, jnp.where(upper, swapped, v), 0.0))
    hi_o, lo_o = split_rows(jnp.where(keep, jnp.where(upper, v, swapped), 0.0))
    rows = jnp.concatenate([hi_e, hi_o, lo_e, lo_o], axis=0)
    none = jnp.zeros_like(rows)
    return jnp.concatenate([jnp.where(ab_pair == 0, rows, none), jnp.where(ab_pair == 1, rows, none)], axis=1)


def contract_kernel(sources, offsets, fresh, pair, group, *refs):
    count, blocks_held = len(sources), len(offsets)
    place, spots = refs[:2]
    t_tiles = refs[2 : 2 + blocks_held]
    shares = refs[2 + blocks_held : 2 + blocks_held + count]
    rest = refs[2 + blocks_held + count :]
    sums = None if fresh else rest[0]
    out = rest[-1]
    layer = place[1]
    blocks, ij = out.shape[1:3]
    rows = pair * HALF
    cols = spots.shape[1] // pair
    columns = [((place[0] + shift) & (cols - 1)) ^ flip for _, shift, flip in sources]
    members = [place[2] ^ offset for offset in offsets]
    for block in range(blocks):
        used = [
            n for n in range(count)
            if sources[n][0] <= block < sources[n][0] + shares[n].shape[0] // (group * rows)
        ]
        total = None
        for n in used:
            for held in range(blocks_held):
                first = pl.multiple_of(((block - sources[n][0]) * group + members[held]) * rows, rows)
                left, right = [], []
                for p in range(pair):
                    spot = spots[block * group + members[held], columns[n] * pair + p]
                    left.append(t_tiles[held][jnp.maximum(spot, 0) >> 2])
                    right.append(slot_rows(shares[n][pl.ds(first + p * HALF, HALF), :], spot))
                part = jnp.dot(
                    jnp.concatenate(left, axis=1),
                    jnp.concatenate(right, axis=0),
                    preferred_element_type=jnp.float32,
                )
                total = part if total is None else total + part
        total = total[:ij] + total[ij:]
        mine = total[:, :LANES]
        other = total[:, LANES:]
        if sums is not None:
            mine = mine + sums[layer, block]
            other = other + sums[1 - layer, block]
        out[layer, block] = mine
        out[1 - layer, block] = other


def contract(sums, place, spots, held, shares, pair):
    group = GROUP
    blocks = spots.shape[0] // group
    ij = next(iter(held.values())).shape[1] // 2
    sources = tuple(source for source, _ in shares)
    offsets = tuple(held)
    given = [place, spots, *held.values(), *(share for _, share in shares)]
    specs = [SMEM, SMEM] + [VMEM] * (len(given) - 2)
    if sums is not None:
        given.append(sums)
        specs.append(VMEM)

    def kernel(*refs):
        contract_kernel(sources, offsets, sums is None, pair, group, *refs)

    return pl.pallas_call(
        kernel,
        out_shape=jax.ShapeDtypeStruct((2, blocks, ij, LANES), jnp.float32),
        in_specs=specs,
        out_specs=VMEM,
        input_output_aliases={} if sums is None else {len(given) - 1: 0},
        compiler_params=pltpu.CompilerParams(vmem_limit_bytes=14 * 2**20),
        cost_estimate=pl.CostEstimate(
            flops=2**20,
            bytes_accessed=2**16,
            transcendentals=0,
        ),
    )(*given)


def on_device(t_amps, v_tiles, v_where):
    cols = lax.axis_size("col")
    rows_axis = lax.axis_size("row")
    held, slots = v_tiles.shape[0], v_tiles.shape[3]
    pair = slots // cols
    rows = pair * HALF
    blocks = rows_axis // GROUP
    ranks = [
        [2 * (GROUP * m + (m.bit_count() + odd) % 2) + x for m in range(blocks // 2) for x in range(2)]
        for odd in range(2)
    ]
    place = jnp.stack([lax.axis_index("col"), lax.axis_index("layer"), lax.axis_index("row") // 2 % GROUP])

    def send(share, to, axis="col", size=cols):
        return lax.ppermute(share, axis, [(i, to(i)) for i in range(size)])

    def send_t(t_block):
        return send(t_block, lambda i: i ^ 2, "row", rows_axis)

    parts = pack(v_tiles, v_where, cols)
    parts = lax.all_to_all(parts, "col", 0, 0, tiled=True)
    parts = parts.reshape(blocks // 2, GROUP, 2, rows + 8, LANES).transpose(0, 2, 1, 3, 4)
    parts = parts.reshape(blocks, GROUP * (rows + 8), LANES)
    parts = lax.all_to_all(parts, "row", 0, 0, tiled=True, axis_index_groups=ranks)
    parts = parts.reshape(blocks * GROUP, rows + 8, LANES)
    spots = parts[:, rows, :slots].astype(jnp.int32)
    own = parts[:, :rows].reshape(blocks * GROUP * rows, LANES)
    own, t_other = lax.optimization_barrier((own, t_amps))

    def up(i):
        return (i + 2) % cols

    def down(i):
        return (i - 2) % cols

    def across(i):
        return i ^ 1

    def add(sums, held, *shares):
        return contract(sums, place, spots, held, shares, pair)

    half, middle = own.shape[0] // 2, blocks // 2
    partner = send(own, across)
    below = send(own, up)
    above = send(own, down)
    t_other = send_t(t_other)
    tiles = {0: prepare(t_amps)}
    sums = add(None, tiles, ((0, 0, 0), own))
    sums, partner, below, above = lax.optimization_barrier((sums, partner, below, above))
    far_low = send(below[:half], up)
    far_high = send(above[half:], down)
    partner_below = send(partner, up)
    partner_above = send(partner, down)
    near = [((0, 0, 0), own), ((0, 0, 1), partner), ((0, -2, 0), below), ((0, 2, 0), above)]
    sums = add(sums, tiles, *near[1:])
    sums, far_low, far_high = lax.optimization_barrier((sums, far_low, far_high))
    partner_far_low = send(far_low, across)
    partner_far_high = send(far_high, across)
    other = {1: prepare(t_other)}
    sums = add(sums, other, *near)
    both = {**tiles, **other}
    sums = add(sums, both, ((0, 4, 0), far_low), ((middle, 4, 0), far_high))
    sums = add(sums, both, ((0, -2, 1), partner_below), ((0, 2, 1), partner_above))
    sums = add(sums, both, ((0, 4, 1), partner_far_low), ((middle, 4, 1), partner_far_high))

    sums = sums[0] + lax.ppermute(sums[1], "layer", [(0, 1), (1, 0)])
    sums = lax.all_to_all(sums, "row", 0, 0, tiled=True, axis_index_groups=ranks)
    return jnp.sum(sums, axis=0)


def solution(mesh):
    return jax.shard_map(
        on_device,
        mesh=mesh,
        in_specs=(
            P("col", ("row", "layer")),
            P("col", "layer", "row", None, None),
            P("col", "layer", "row", None),
        ),
        out_specs=P("col", ("row", "layer")),
        check_vma=False,
    )
```

```python
import jax
import jax.numpy as jnp
from jax import lax
from jax.experimental import pallas as pl
from jax.experimental.pallas import tpu as pltpu
from jax.sharding import PartitionSpec as P

TILE = 64
AB_DEV = 128
LANES = 128
GROUP = 4
HALF = TILE // 2
VMEM = pl.BlockSpec(memory_space=pltpu.VMEM)
SMEM = pl.BlockSpec(memory_space=pltpu.SMEM)


def split_rows(x):
    hi = x.astype(jnp.bfloat16)
    return hi, (x - hi.astype(jnp.float32)).astype(jnp.bfloat16)


def pack_kernel(spots, lists, out):
    held, slots = spots.shape
    cols = out.shape[0]
    pair = slots // cols
    rows = pair * HALF
    lane = lax.broadcasted_iota(jnp.int32, (8, LANES), 1)
    for b in range(held):
        row = jnp.zeros((8, LANES), jnp.float32)
        for s in range(slots):
            row = jnp.where(lane == s, spots[b, s].astype(jnp.float32), row)
        base = b * (rows + 8)
        for c in range(cols):
            for p in range(pair):
                s = c * pair + p
                out[c, base + p * HALF : base + (p + 1) * HALF] = lists[b, s // 8, pl.ds(s % 8, HALF, stride=8), :]
            out[c, base + rows : base + rows + 8] = row


def pack(v_tiles, v_where, cols):
    held, slots = v_tiles.shape[0], v_tiles.shape[3]
    lists = v_tiles.reshape(held, slots // 8, 8, HALF, LANES).transpose(0, 1, 3, 2, 4)
    lists = lists.reshape(held, slots // 8, HALF * 8, LANES)
    return pl.pallas_call(
        pack_kernel,
        out_shape=jax.ShapeDtypeStruct((cols, held * (slots // cols * HALF + 8), LANES), jnp.float32),
        in_specs=[SMEM, VMEM],
        out_specs=VMEM,
        compiler_params=pltpu.CompilerParams(vmem_limit_bytes=14 * 2**20),
        cost_estimate=pl.CostEstimate(flops=0, bytes_accessed=2**20, transcendentals=0),
    )(v_where.reshape(held, slots), lists)


def prepare_kernel(*refs):
    *halves, t_tiles = refs
    row = lax.broadcasted_iota(jnp.int32, (LANES, 2 * LANES), 0)
    col = lax.broadcasted_iota(jnp.int32, (LANES, 2 * LANES), 1)
    source = (col // LANES) * TILE + 2 * (col % HALF) + (col % TILE) // HALF
    pick = (row == source).astype(jnp.bfloat16)
    for at in range(halves[0].shape[1] // LANES):
        split = [split_rows(half[:, at * LANES : (at + 1) * LANES]) for half in halves]
        rows = jnp.concatenate([hi for hi, _ in split] + [lo for _, lo in split], axis=0)
        both = jnp.dot(rows, pick, preferred_element_type=jnp.float32).astype(jnp.bfloat16)
        t_tiles[2 * at] = both[:, :LANES]
        t_tiles[2 * at + 1] = both[:, LANES:]


def prepare(*halves):
    ij, cd = sum(half.shape[0] for half in halves), halves[0].shape[1]
    return pl.pallas_call(
        prepare_kernel,
        out_shape=jax.ShapeDtypeStruct((cd // TILE, 2 * ij, LANES), jnp.bfloat16),
        in_specs=[VMEM] * len(halves),
        out_specs=VMEM,
        compiler_params=pltpu.CompilerParams(vmem_limit_bytes=14 * 2**20),
        cost_estimate=pl.CostEstimate(flops=2 * 2 * ij * cd * 2 * LANES, bytes_accessed=3 * 2**20, transcendentals=0),
    )(*halves)


def slot_rows(v, spot):
    lane_half = lax.broadcasted_iota(jnp.int32, (HALF, LANES), 1) // TILE
    safe = jnp.maximum(spot, 0)
    ab_half = safe & 1
    ab_pair = (safe >> 1) & 1
    swapped = pltpu.roll(v, TILE, 1)
    upper = ab_half == 1
    keep = (lane_half == ab_half) & (spot >= 0)
    hi_e, lo_e = split_rows(jnp.where(keep, jnp.where(upper, swapped, v), 0.0))
    hi_o, lo_o = split_rows(jnp.where(keep, jnp.where(upper, v, swapped), 0.0))
    rows = jnp.concatenate([hi_e, hi_o, lo_e, lo_o], axis=0)
    none = jnp.zeros_like(rows)
    return jnp.concatenate([jnp.where(ab_pair == 0, rows, none), jnp.where(ab_pair == 1, rows, none)], axis=1)


def contract_kernel(sources, offsets, fresh, pair, group, *refs):
    count, blocks_held = len(sources), len(offsets)
    place, spots = refs[:2]
    t_tiles = refs[2 : 2 + blocks_held]
    shares = refs[2 + blocks_held : 2 + blocks_held + count]
    rest = refs[2 + blocks_held + count :]
    sums = None if fresh else rest[0]
    out = rest[-1]
    layer = place[1]
    blocks, ij = out.shape[1:3]
    rows = pair * HALF
    cols = spots.shape[1] // pair
    columns = [((place[0] + shift) & (cols - 1)) ^ flip for _, shift, flip in sources]
    members = [place[2] ^ offset for offset in offsets]
    for block in range(blocks):
        used = [
            n for n in range(count)
            if sources[n][0] <= block < sources[n][0] + shares[n].shape[0] // (group * rows)
        ]
        total = None
        for n in used:
            for held in range(blocks_held):
                first = pl.multiple_of(((block - sources[n][0]) * group + members[held]) * rows, rows)
                left, right = [], []
                for p in range(pair):
                    spot = spots[block * group + members[held], columns[n] * pair + p]
                    left.append(t_tiles[held][jnp.maximum(spot, 0) >> 2])
                    right.append(slot_rows(shares[n][pl.ds(first + p * HALF, HALF), :], spot))
                part = jnp.dot(
                    jnp.concatenate(left, axis=1),
                    jnp.concatenate(right, axis=0),
                    preferred_element_type=jnp.float32,
                )
                total = part if total is None else total + part
        total = total[:ij] + total[ij:]
        mine = total[:, :LANES]
        other = total[:, LANES:]
        if sums is not None:
            mine = mine + sums[layer, block]
            other = other + sums[1 - layer, block]
        out[layer, block] = mine
        out[1 - layer, block] = other


def contract(sums, place, spots, held, shares, pair):
    group = GROUP
    blocks = spots.shape[0] // group
    ij = next(iter(held.values())).shape[1] // 2
    sources = tuple(source for source, _ in shares)
    offsets = tuple(held)
    given = [place, spots, *held.values(), *(share for _, share in shares)]
    specs = [SMEM, SMEM] + [VMEM] * (len(given) - 2)
    if sums is not None:
        given.append(sums)
        specs.append(VMEM)

    def kernel(*refs):
        contract_kernel(sources, offsets, sums is None, pair, group, *refs)

    return pl.pallas_call(
        kernel,
        out_shape=jax.ShapeDtypeStruct((2, blocks, ij, LANES), jnp.float32),
        in_specs=specs,
        out_specs=VMEM,
        input_output_aliases={} if sums is None else {len(given) - 1: 0},
        compiler_params=pltpu.CompilerParams(vmem_limit_bytes=14 * 2**20),
        cost_estimate=pl.CostEstimate(
            flops=2**12,
            bytes_accessed=2**10,
            transcendentals=0,
        ),
    )(*given)


def sort_kernel(rows, slots, place, parts, *chunks):
    m = place[3]
    for k in range(len(chunks)):
        for n in range(GROUP):
            base = n * (rows + 8)
            chunks[k][n * rows : (n + 1) * rows] = parts[m ^ k, base : base + rows]
        at = lax.broadcasted_iota(jnp.int32, (8, LANES), 0)
        spots = jnp.zeros((8, LANES), jnp.float32)
        for n in range(GROUP):
            base = n * (rows + 8) + rows
            spots = jnp.where(at == n, parts[m ^ k, base : base + 8], spots)
        chunks[k][GROUP * rows :] = spots


def sort(place, parts, blocks, rows, slots):
    def kernel(*refs):
        sort_kernel(rows, slots, *refs)

    return pl.pallas_call(
        kernel,
        out_shape=[jax.ShapeDtypeStruct((GROUP * rows + 8, LANES), jnp.float32)] * blocks,
        in_specs=[SMEM, VMEM],
        out_specs=[VMEM] * blocks,
        compiler_params=pltpu.CompilerParams(vmem_limit_bytes=14 * 2**20),
        cost_estimate=pl.CostEstimate(flops=0, bytes_accessed=2**16, transcendentals=0),
    )(place, parts)


def join_kernel(*refs):
    *chunks, own, spots = refs
    for k, chunk in enumerate(chunks):
        size = chunk.shape[0] - 8
        own[k * size : (k + 1) * size] = chunk[:size]
        spots[k] = chunk[size:].astype(jnp.int32)


def join(chunks):
    size = chunks[0].shape[0] - 8
    return pl.pallas_call(
        join_kernel,
        out_shape=[
            jax.ShapeDtypeStruct((len(chunks) * size, LANES), jnp.float32),
            jax.ShapeDtypeStruct((len(chunks), 8, LANES), jnp.int32),
        ],
        in_specs=[VMEM] * len(chunks),
        out_specs=[VMEM] * 2,
        compiler_params=pltpu.CompilerParams(vmem_limit_bytes=14 * 2**20),
        cost_estimate=pl.CostEstimate(flops=0, bytes_accessed=2**16, transcendentals=0),
    )(*chunks)


def on_device(t_amps, v_tiles, v_where):
    cols = lax.axis_size("col")
    rows_axis = lax.axis_size("row")
    slots = v_tiles.shape[3]
    pair = slots // cols
    rows = pair * HALF
    blocks = rows_axis // GROUP
    row = lax.axis_index("row")
    place = jnp.stack([lax.axis_index("col"), lax.axis_index("layer"), row % GROUP, row // GROUP])

    def send(share, to, axis="col", size=cols):
        return lax.ppermute(share, axis, [(i, to(i)) for i in range(size)])

    def send_t(t_block, offset):
        return send(t_block, lambda i: i ^ offset, "row", rows_axis)

    def send_m(chunk, k):
        def to(i):
            return i ^ (GROUP * k) ^ (2 * (k.bit_count() % 2))

        return send(chunk, to, "row", rows_axis)

    t_one, t_two = send_t(t_amps, 1), send_t(t_amps, 2)
    parts = pack(v_tiles, v_where, cols)
    parts = lax.all_to_all(parts, "col", 0, 0, tiled=True)
    parts, t_two = lax.optimization_barrier((parts, t_two))
    parts = parts.reshape(blocks, GROUP * (rows + 8), LANES)
    chunks = sort(place, parts, blocks, rows, slots)
    chunks = [chunks[0]] + [send_m(chunks[k], k) for k in range(1, blocks)]
    own, spots = join(chunks)
    spots = spots[:, :GROUP, :slots].reshape(blocks * GROUP, slots)
    own, t_one = lax.optimization_barrier((own, t_one))

    def up(i):
        return (i + 2) % cols

    def down(i):
        return (i - 2) % cols

    def across(i):
        return i ^ 1

    def add(sums, held, *shares):
        return contract(sums, place, spots, held, shares, pair)

    half, middle = own.shape[0] // 2, blocks // 2
    partner = send(own, across)
    below = send(own, up)
    above = send(own, down)
    t_three = send_t(t_one, 2)
    early = {0: prepare(t_amps), 2: prepare(t_two)}
    sums = add(None, early, ((0, 0, 0), own))
    sums, partner, below, above = lax.optimization_barrier((sums, partner, below, above))
    far_low = send(below[:half], up)
    far_high = send(above[half:], down)
    partner_below = send(partner, up)
    partner_above = send(partner, down)
    near = [((0, 0, 0), own), ((0, 0, 1), partner), ((0, -2, 0), below), ((0, 2, 0), above)]
    sums = add(sums, early, *near[1:])
    sums, far_low, far_high = lax.optimization_barrier((sums, far_low, far_high))
    partner_far_low = send(far_low, across)
    partner_far_high = send(far_high, across)
    one = {1: prepare(t_one)}
    most = {**early, **one}
    far = [((0, 4, 0), far_low), ((middle, 4, 0), far_high)]
    beside = [((0, -2, 1), partner_below), ((0, 2, 1), partner_above)]
    last = [((0, 4, 1), partner_far_low), ((middle, 4, 1), partner_far_high)]
    sums = add(sums, one, *near)
    sums = add(sums, most, *far)
    sums = add(sums, most, *beside)
    sums, t_three = lax.optimization_barrier((sums, t_three))
    three = {3: prepare(t_three)}
    sums = add(sums, three, *near, *far, *beside)
    sums = add(sums, {**most, **three}, *last)

    sums = sums[0] + lax.ppermute(sums[1], "layer", [(0, 1), (1, 0)])
    received = [send_m(sums[k], k) for k in range(1, blocks)]
    return sum(received, sums[0])


def solution(mesh):
    return jax.shard_map(
        on_device,
        mesh=mesh,
        in_specs=(
            P("col", ("row", "layer")),
            P("col", "layer", "row", None, None),
            P("col", "layer", "row", None),
        ),
        out_specs=P("col", ("row", "layer")),
        check_vma=False,
    )
```

```python
import jax
import jax.numpy as jnp
from jax import lax
from jax.experimental import pallas as pl
from jax.experimental.pallas import tpu as pltpu
from jax.sharding import PartitionSpec as P

TILE = 64
AB_DEV = 128
LANES = 128
GROUP = 2
HALF = TILE // 2
VMEM = pl.BlockSpec(memory_space=pltpu.VMEM)
SMEM = pl.BlockSpec(memory_space=pltpu.SMEM)


def split_rows(x):
    hi = x.astype(jnp.bfloat16)
    return hi, (x - hi.astype(jnp.float32)).astype(jnp.bfloat16)


def pack_kernel(spots, lists, out):
    held, slots = spots.shape
    cols = out.shape[0]
    pair = slots // cols
    rows = pair * HALF
    lane = lax.broadcasted_iota(jnp.int32, (8, LANES), 1)
    for b in range(held):
        row = jnp.zeros((8, LANES), jnp.float32)
        for s in range(slots):
            row = jnp.where(lane == s, spots[b, s].astype(jnp.float32), row)
        base = b * (rows + 8)
        for c in range(cols):
            for p in range(pair):
                s = c * pair + p
                out[c, base + p * HALF : base + (p + 1) * HALF] = lists[b, s // 8, pl.ds(s % 8, HALF, stride=8), :]
            out[c, base + rows : base + rows + 8] = row


def pack(v_tiles, v_where, cols):
    held, slots = v_tiles.shape[0], v_tiles.shape[3]
    lists = v_tiles.reshape(held, slots // 8, 8, HALF, LANES).transpose(0, 1, 3, 2, 4)
    lists = lists.reshape(held, slots // 8, HALF * 8, LANES)
    return pl.pallas_call(
        pack_kernel,
        out_shape=jax.ShapeDtypeStruct((cols, held * (slots // cols * HALF + 8), LANES), jnp.float32),
        in_specs=[SMEM, VMEM],
        out_specs=VMEM,
        compiler_params=pltpu.CompilerParams(vmem_limit_bytes=14 * 2**20),
        cost_estimate=pl.CostEstimate(flops=0, bytes_accessed=2**20, transcendentals=0),
    )(v_where.reshape(held, slots), lists)


def prepare_kernel(*refs):
    *halves, t_tiles = refs
    row = lax.broadcasted_iota(jnp.int32, (LANES, 2 * LANES), 0)
    col = lax.broadcasted_iota(jnp.int32, (LANES, 2 * LANES), 1)
    source = (col // LANES) * TILE + 2 * (col % HALF) + (col % TILE) // HALF
    pick = (row == source).astype(jnp.bfloat16)
    for at in range(halves[0].shape[1] // LANES):
        split = [split_rows(half[:, at * LANES : (at + 1) * LANES]) for half in halves]
        rows = jnp.concatenate([hi for hi, _ in split] + [lo for _, lo in split], axis=0)
        both = jnp.dot(rows, pick, preferred_element_type=jnp.float32).astype(jnp.bfloat16)
        t_tiles[2 * at] = both[:, :LANES]
        t_tiles[2 * at + 1] = both[:, LANES:]


def prepare(*halves):
    ij, cd = sum(half.shape[0] for half in halves), halves[0].shape[1]
    return pl.pallas_call(
        prepare_kernel,
        out_shape=jax.ShapeDtypeStruct((cd // TILE, 2 * ij, LANES), jnp.bfloat16),
        in_specs=[VMEM] * len(halves),
        out_specs=VMEM,
        compiler_params=pltpu.CompilerParams(vmem_limit_bytes=14 * 2**20),
        cost_estimate=pl.CostEstimate(flops=2 * 2 * ij * cd * 2 * LANES, bytes_accessed=3 * 2**20, transcendentals=0),
    )(*halves)


def slot_rows(v, spot):
    lane_half = lax.broadcasted_iota(jnp.int32, (HALF, LANES), 1) // TILE
    safe = jnp.maximum(spot, 0)
    ab_half = safe & 1
    ab_pair = (safe >> 1) & 1
    swapped = pltpu.roll(v, TILE, 1)
    upper = ab_half == 1
    keep = (lane_half == ab_half) & (spot >= 0)
    hi_e, lo_e = split_rows(jnp.where(keep, jnp.where(upper, swapped, v), 0.0))
    hi_o, lo_o = split_rows(jnp.where(keep, jnp.where(upper, v, swapped), 0.0))
    rows = jnp.concatenate([hi_e, hi_o, lo_e, lo_o], axis=0)
    none = jnp.zeros_like(rows)
    return jnp.concatenate([jnp.where(ab_pair == 0, rows, none), jnp.where(ab_pair == 1, rows, none)], axis=1)


def contract_kernel(sources, offsets, fresh, pair, group, *refs):
    count, blocks_held = len(sources), len(offsets)
    place, spots = refs[:2]
    t_tiles = refs[2 : 2 + blocks_held]
    shares = refs[2 + blocks_held : 2 + blocks_held + count]
    rest = refs[2 + blocks_held + count :]
    sums = None if fresh else rest[0]
    out = rest[-1]
    layer = place[1]
    blocks, ij = out.shape[1:3]
    rows = pair * HALF
    cols = spots.shape[1] // pair
    columns = [((place[0] + shift) & (cols - 1)) ^ flip for _, shift, flip in sources]
    members = [place[2] ^ offset for offset in offsets]
    for block in range(blocks):
        used = [
            n for n in range(count)
            if sources[n][0] <= block < sources[n][0] + shares[n].shape[0] // (group * rows)
        ]
        total = None
        for n in used:
            for held in range(blocks_held):
                first = pl.multiple_of(((block - sources[n][0]) * group + members[held]) * rows, rows)
                left, right = [], []
                for p in range(pair):
                    spot = spots[block * group + members[held], columns[n] * pair + p]
                    left.append(t_tiles[held][jnp.maximum(spot, 0) >> 2])
                    right.append(slot_rows(shares[n][pl.ds(first + p * HALF, HALF), :], spot))
                part = jnp.dot(
                    jnp.concatenate(left, axis=1),
                    jnp.concatenate(right, axis=0),
                    preferred_element_type=jnp.float32,
                )
                total = part if total is None else total + part
        total = total[:ij] + total[ij:]
        mine = total[:, :LANES]
        other = total[:, LANES:]
        to = place[3] ^ block
        if sums is not None:
            mine = mine + sums[layer, to]
            other = other + sums[1 - layer, to]
        out[layer, to] = mine
        out[1 - layer, to] = other


def contract(sums, place, spots, held, shares, pair):
    group = GROUP
    blocks = spots.shape[0] // group
    ij = next(iter(held.values())).shape[1] // 2
    sources = tuple(source for source, _ in shares)
    offsets = tuple(held)
    given = [place, spots, *held.values(), *(share for _, share in shares)]
    specs = [SMEM, SMEM] + [VMEM] * (len(given) - 2)
    if sums is not None:
        given.append(sums)
        specs.append(VMEM)

    def kernel(*refs):
        contract_kernel(sources, offsets, sums is None, pair, group, *refs)

    return pl.pallas_call(
        kernel,
        out_shape=jax.ShapeDtypeStruct((2, blocks, ij, LANES), jnp.float32),
        in_specs=specs,
        out_specs=VMEM,
        input_output_aliases={} if sums is None else {len(given) - 1: 0},
        compiler_params=pltpu.CompilerParams(vmem_limit_bytes=14 * 2**20),
        cost_estimate=pl.CostEstimate(
            flops=2**20,
            bytes_accessed=2**16,
            transcendentals=0,
        ),
    )(*given)


def sort_kernel(rows, place, parts, *chunks):
    for n in range(len(chunks)):
        to = place[3] ^ n
        base = pl.multiple_of((to & 1) * (rows + 8), 8)
        at = lax.broadcasted_iota(jnp.int32, (8, LANES), 0)
        spots = jnp.zeros((8, LANES), jnp.float32)
        for e in range(GROUP):
            source = (to >> 1) * GROUP + e
            chunks[n][e * rows : (e + 1) * rows] = parts[source, pl.ds(base, rows), :]
            spots = jnp.where(at == e, parts[source, pl.ds(base + rows, 8), :], spots)
        chunks[n][GROUP * rows :] = spots


def sort(place, parts, blocks, rows):
    def kernel(*refs):
        sort_kernel(rows, *refs)

    return pl.pallas_call(
        kernel,
        out_shape=[jax.ShapeDtypeStruct((GROUP * rows + 8, LANES), jnp.float32)] * blocks,
        in_specs=[SMEM, VMEM],
        out_specs=[VMEM] * blocks,
        compiler_params=pltpu.CompilerParams(vmem_limit_bytes=14 * 2**20),
        cost_estimate=pl.CostEstimate(flops=0, bytes_accessed=2**16, transcendentals=0),
    )(place, parts)


def join_kernel(*refs):
    *chunks, own, spots = refs
    for k, chunk in enumerate(chunks):
        size = chunk.shape[0] - 8
        own[k * size : (k + 1) * size] = chunk[:size]
        spots[k] = chunk[size:].astype(jnp.int32)


def join(chunks):
    size = chunks[0].shape[0] - 8
    return pl.pallas_call(
        join_kernel,
        out_shape=[
            jax.ShapeDtypeStruct((len(chunks) * size, LANES), jnp.float32),
            jax.ShapeDtypeStruct((len(chunks), 8, LANES), jnp.int32),
        ],
        in_specs=[VMEM] * len(chunks),
        out_specs=[VMEM] * 2,
        compiler_params=pltpu.CompilerParams(vmem_limit_bytes=14 * 2**20),
        cost_estimate=pl.CostEstimate(flops=0, bytes_accessed=2**16, transcendentals=0),
    )(*chunks)


def on_device(t_amps, v_tiles, v_where):
    cols = lax.axis_size("col")
    rows_axis = lax.axis_size("row")
    held, slots = v_tiles.shape[0], v_tiles.shape[3]
    pair = slots // cols
    rows = pair * HALF
    blocks = rows_axis // GROUP
    ranks = [
        [2 * (GROUP * m + (m.bit_count() + odd) % 2) + x for m in range(blocks // 2) for x in range(2)]
        for odd in range(2)
    ]
    row = lax.axis_index("row")
    place = jnp.stack(
        [lax.axis_index("col"), lax.axis_index("layer"), row // 2 % GROUP, row // (2 * GROUP) * 2 + row % 2]
    )

    def send(share, to, axis="col", size=cols):
        return lax.ppermute(share, axis, [(i, to(i)) for i in range(size)])

    def send_t(t_block):
        return send(t_block, lambda i: i ^ 2, "row", rows_axis)

    parts = pack(v_tiles, v_where, cols)
    parts = lax.all_to_all(parts, "col", 0, 0, tiled=True)
    chunks = sort(place, parts, blocks, rows)

    def send_block(chunk, n):
        m, x = n // 2, n % 2
        return send(chunk, lambda i: i ^ (2 * GROUP * m) ^ (2 * (m.bit_count() % 2)) ^ x, "row", rows_axis)

    own, spots = join([chunks[0]] + [send_block(chunks[n], n) for n in range(1, blocks)])
    spots = spots[:, :GROUP, :slots].reshape(blocks * GROUP, slots)
    own, t_other = lax.optimization_barrier((own, t_amps))

    def up(i):
        return (i + 2) % cols

    def down(i):
        return (i - 2) % cols

    def across(i):
        return i ^ 1

    def add(sums, held, *shares):
        return contract(sums, place, spots, held, shares, pair)

    half, middle = own.shape[0] // 2, blocks // 2
    partner = send(own, across)
    below = send(own, up)
    above = send(own, down)
    t_other = send_t(t_other)
    tiles = {0: prepare(t_amps)}
    sums = add(None, tiles, ((0, 0, 0), own))
    sums, partner, below, above = lax.optimization_barrier((sums, partner, below, above))
    far_low = send(below[:half], up)
    far_high = send(above[half:], down)
    partner_below = send(partner, up)
    partner_above = send(partner, down)
    near = [((0, 0, 0), own), ((0, 0, 1), partner), ((0, -2, 0), below), ((0, 2, 0), above)]
    sums = add(sums, tiles, *near[1:])
    sums, far_low, far_high = lax.optimization_barrier((sums, far_low, far_high))
    partner_far_low = send(far_low, across)
    partner_far_high = send(far_high, across)
    other = {1: prepare(t_other)}
    sums = add(sums, other, *near)
    both = {**tiles, **other}
    sums = add(sums, both, ((0, 4, 0), far_low), ((middle, 4, 0), far_high))
    sums = add(sums, both, ((0, -2, 1), partner_below), ((0, 2, 1), partner_above))
    sums = add(sums, both, ((0, 4, 1), partner_far_low), ((middle, 4, 1), partner_far_high))

    sums = sums[0] + lax.ppermute(sums[1], "layer", [(0, 1), (1, 0)])
    sums = lax.all_to_all(sums, "row", 0, 0, tiled=True, axis_index_groups=ranks)
    return jnp.sum(sums, axis=0)


def solution(mesh):
    return jax.shard_map(
        on_device,
        mesh=mesh,
        in_specs=(
            P("col", ("row", "layer")),
            P("col", "layer", "row", None, None),
            P("col", "layer", "row", None),
        ),
        out_specs=P("col", ("row", "layer")),
        check_vma=False,
    )
```

```python
import jax
import jax.numpy as jnp
from jax import lax
from jax.experimental import pallas as pl
from jax.experimental.pallas import tpu as pltpu
from jax.sharding import PartitionSpec as P

TILE = 64
AB_DEV = 128
LANES = 128
GROUP = 2
HALF = TILE // 2
VMEM = pl.BlockSpec(memory_space=pltpu.VMEM)
SMEM = pl.BlockSpec(memory_space=pltpu.SMEM)


def split_rows(x):
    hi = x.astype(jnp.bfloat16)
    return hi, (x - hi.astype(jnp.float32)).astype(jnp.bfloat16)


def pack_kernel(spots, lists, out):
    held, slots = spots.shape
    cols = out.shape[0] // held
    pair = slots // cols
    rows = pair * HALF
    lane = lax.broadcasted_iota(jnp.int32, (8, LANES), 1)
    for b in range(held):
        row = jnp.zeros((8, LANES), jnp.float32)
        for s in range(slots):
            row = jnp.where(lane == s, spots[b, s].astype(jnp.float32), row)
        for c in range(cols):
            for p in range(pair):
                s = c * pair + p
                out[b * cols + c, p * HALF : (p + 1) * HALF] = lists[b, s // 8, pl.ds(s % 8, HALF, stride=8), :]
            out[b * cols + c, rows:] = row


def pack(v_tiles, v_where, cols):
    held, slots = v_tiles.shape[0], v_tiles.shape[3]
    lists = v_tiles.reshape(held, slots // 8, 8, HALF, LANES).transpose(0, 1, 3, 2, 4)
    lists = lists.reshape(held, slots // 8, HALF * 8, LANES)
    return pl.pallas_call(
        pack_kernel,
        out_shape=jax.ShapeDtypeStruct((held * cols, slots // cols * HALF + 8, LANES), jnp.float32),
        in_specs=[SMEM, VMEM],
        out_specs=VMEM,
        compiler_params=pltpu.CompilerParams(vmem_limit_bytes=14 * 2**20),
        cost_estimate=pl.CostEstimate(flops=0, bytes_accessed=2**20, transcendentals=0),
    )(v_where.reshape(held, slots), lists)


def prepare_kernel(*refs):
    *halves, t_tiles = refs
    row = lax.broadcasted_iota(jnp.int32, (LANES, 2 * LANES), 0)
    col = lax.broadcasted_iota(jnp.int32, (LANES, 2 * LANES), 1)
    source = (col // LANES) * TILE + 2 * (col % HALF) + (col % TILE) // HALF
    pick = (row == source).astype(jnp.bfloat16)
    for at in range(halves[0].shape[1] // LANES):
        split = [split_rows(half[:, at * LANES : (at + 1) * LANES]) for half in halves]
        rows = jnp.concatenate([hi for hi, _ in split] + [lo for _, lo in split], axis=0)
        both = jnp.dot(rows, pick, preferred_element_type=jnp.float32).astype(jnp.bfloat16)
        t_tiles[2 * at] = both[:, :LANES]
        t_tiles[2 * at + 1] = both[:, LANES:]


def prepare(*halves):
    ij, cd = sum(half.shape[0] for half in halves), halves[0].shape[1]
    return pl.pallas_call(
        prepare_kernel,
        out_shape=jax.ShapeDtypeStruct((cd // TILE, 2 * ij, LANES), jnp.bfloat16),
        in_specs=[VMEM] * len(halves),
        out_specs=VMEM,
        compiler_params=pltpu.CompilerParams(vmem_limit_bytes=14 * 2**20),
        cost_estimate=pl.CostEstimate(flops=2 * 2 * ij * cd * 2 * LANES, bytes_accessed=3 * 2**20, transcendentals=0),
    )(*halves)


def slot_rows(v, spot):
    lane_half = lax.broadcasted_iota(jnp.int32, (HALF, LANES), 1) // TILE
    safe = jnp.maximum(spot, 0)
    ab_half = safe & 1
    ab_pair = (safe >> 1) & 1
    swapped = pltpu.roll(v, TILE, 1)
    upper = ab_half == 1
    keep = (lane_half == ab_half) & (spot >= 0)
    hi_e, lo_e = split_rows(jnp.where(keep, jnp.where(upper, swapped, v), 0.0))
    hi_o, lo_o = split_rows(jnp.where(keep, jnp.where(upper, v, swapped), 0.0))
    rows = jnp.concatenate([hi_e, hi_o, lo_e, lo_o], axis=0)
    none = jnp.zeros_like(rows)
    return jnp.concatenate([jnp.where(ab_pair == 0, rows, none), jnp.where(ab_pair == 1, rows, none)], axis=1)


def contract_kernel(sources, offsets, fresh, pair, group, *refs):
    count, blocks_held = len(sources), len(offsets)
    place, spots = refs[:2]
    t_tiles = refs[2 : 2 + blocks_held]
    shares = refs[2 + blocks_held : 2 + blocks_held + count]
    rest = refs[2 + blocks_held + count :]
    sums = None if fresh else rest[0]
    out = rest[-1]
    layer = place[1]
    blocks, ij = out.shape[1:3]
    rows = pair * HALF
    cols = spots.shape[1] // pair
    columns = [((place[0] + shift) & (cols - 1)) ^ flip for _, shift, flip in sources]
    members = [place[2] ^ offset for offset in offsets]
    for block in range(blocks):
        used = [
            n for n in range(count)
            if sources[n][0] <= block < sources[n][0] + shares[n].shape[0] // (group * rows)
        ]
        total = None
        for n in used:
            for held in range(blocks_held):
                first = pl.multiple_of(((block - sources[n][0]) * group + members[held]) * rows, rows)
                left, right = [], []
                for p in range(pair):
                    spot = spots[block * group + members[held], columns[n] * pair + p]
                    left.append(t_tiles[held][jnp.maximum(spot, 0) >> 2])
                    right.append(slot_rows(shares[n][pl.ds(first + p * HALF, HALF), :], spot))
                part = jnp.dot(
                    jnp.concatenate(left, axis=1),
                    jnp.concatenate(right, axis=0),
                    preferred_element_type=jnp.float32,
                )
                total = part if total is None else total + part
        total = total[:ij] + total[ij:]
        mine = total[:, :LANES]
        other = total[:, LANES:]
        to = place[3] ^ block
        if sums is not None:
            mine = mine + sums[layer, to]
            other = other + sums[1 - layer, to]
        out[layer, to] = mine
        out[1 - layer, to] = other


def contract(sums, place, spots, held, shares, pair):
    group = GROUP
    blocks = spots.shape[0] // group
    ij = next(iter(held.values())).shape[1] // 2
    sources = tuple(source for source, _ in shares)
    offsets = tuple(held)
    given = [place, spots, *held.values(), *(share for _, share in shares)]
    specs = [SMEM, SMEM] + [VMEM] * (len(given) - 2)
    if sums is not None:
        given.append(sums)
        specs.append(VMEM)

    def kernel(*refs):
        contract_kernel(sources, offsets, sums is None, pair, group, *refs)

    return pl.pallas_call(
        kernel,
        out_shape=jax.ShapeDtypeStruct((2, blocks, ij, LANES), jnp.float32),
        in_specs=specs,
        out_specs=VMEM,
        input_output_aliases={} if sums is None else {len(given) - 1: 0},
        compiler_params=pltpu.CompilerParams(vmem_limit_bytes=14 * 2**20),
        cost_estimate=pl.CostEstimate(
            flops=2**20,
            bytes_accessed=2**16,
            transcendentals=0,
        ),
    )(*given)


def sort_kernel(place, parts, *chunks):
    cols = parts.shape[0] // 2
    rows = parts.shape[1] - 8
    for k in range(len(chunks)):
        first = ((place[3] >> 1) ^ k) * GROUP
        at = lax.broadcasted_iota(jnp.int32, (8, LANES), 0)
        spots = jnp.zeros((8, LANES), jnp.float32)
        for x in range(2):
            for e in range(GROUP):
                n, source = x * GROUP + e, x * cols + first + e
                chunks[k][n * rows : (n + 1) * rows] = parts[source, :rows]
                spots = jnp.where(at == n, parts[source, rows:], spots)
        chunks[k][2 * GROUP * rows :] = spots


def sort(place, parts, count):
    rows = parts.shape[1] - 8
    return pl.pallas_call(
        sort_kernel,
        out_shape=[jax.ShapeDtypeStruct((2 * GROUP * rows + 8, LANES), jnp.float32)] * count,
        in_specs=[SMEM, VMEM],
        out_specs=[VMEM] * count,
        compiler_params=pltpu.CompilerParams(vmem_limit_bytes=14 * 2**20),
        cost_estimate=pl.CostEstimate(flops=0, bytes_accessed=2**16, transcendentals=0),
    )(place, parts)


def join_kernel(*refs):
    *chunks, own, spots = refs
    for k, chunk in enumerate(chunks):
        size = chunk.shape[0] - 8
        own[k * size : (k + 1) * size] = chunk[:size]
        spots[k] = chunk[size:].astype(jnp.int32)


def join(chunks):
    size = chunks[0].shape[0] - 8
    return pl.pallas_call(
        join_kernel,
        out_shape=[
            jax.ShapeDtypeStruct((len(chunks) * size, LANES), jnp.float32),
            jax.ShapeDtypeStruct((len(chunks), 8, LANES), jnp.int32),
        ],
        in_specs=[VMEM] * len(chunks),
        out_specs=[VMEM] * 2,
        compiler_params=pltpu.CompilerParams(vmem_limit_bytes=14 * 2**20),
        cost_estimate=pl.CostEstimate(flops=0, bytes_accessed=2**16, transcendentals=0),
    )(*chunks)


def on_device(t_amps, v_tiles, v_where):
    cols = lax.axis_size("col")
    rows_axis = lax.axis_size("row")
    held, slots = v_tiles.shape[0], v_tiles.shape[3]
    pair = slots // cols
    rows = pair * HALF
    blocks = rows_axis // GROUP
    ranks = [
        [2 * (GROUP * m + (m.bit_count() + odd) % 2) + x for m in range(blocks // 2) for x in range(2)]
        for odd in range(2)
    ]
    row = lax.axis_index("row")
    place = jnp.stack(
        [lax.axis_index("col"), lax.axis_index("layer"), row // 2 % GROUP, row // (2 * GROUP) * 2]
    )

    def send(share, to, axis="col", size=cols):
        return lax.ppermute(share, axis, [(i, to(i)) for i in range(size)])

    def send_t(t_block):
        return send(t_block, lambda i: i ^ 2, "row", rows_axis)

    planes = [
        [(2 * z + x) * cols + c for x in range(2) for c in range(cols)] for z in range(rows_axis // 2)
    ]
    parts = pack(v_tiles, v_where, cols)
    parts = lax.all_to_all(parts, ("row", "col"), 0, 0, tiled=True, axis_index_groups=planes)
    chunks = sort(place, parts, blocks // 2)

    def send_m(chunk, k):
        return send(chunk, lambda i: i ^ (2 * GROUP * k) ^ (2 * (k.bit_count() % 2)), "row", rows_axis)

    own, spots = join([chunks[0]] + [send_m(chunks[k], k) for k in range(1, blocks // 2)])
    spots = spots[:, : 2 * GROUP, :slots].reshape(blocks * GROUP, slots)
    own, t_other = lax.optimization_barrier((own, t_amps))

    def up(i):
        return (i + 2) % cols

    def down(i):
        return (i - 2) % cols

    def across(i):
        return i ^ 1

    def add(sums, held, *shares):
        return contract(sums, place, spots, held, shares, pair)

    half, middle = own.shape[0] // 2, blocks // 2
    partner = send(own, across)
    below = send(own, up)
    above = send(own, down)
    t_other = send_t(t_other)
    tiles = {0: prepare(t_amps)}
    sums = add(None, tiles, ((0, 0, 0), own))
    sums, partner, below, above = lax.optimization_barrier((sums, partner, below, above))
    far_low = send(below[:half], up)
    far_high = send(above[half:], down)
    partner_below = send(partner, up)
    partner_above = send(partner, down)
    near = [((0, 0, 0), own), ((0, 0, 1), partner), ((0, -2, 0), below), ((0, 2, 0), above)]
    sums = add(sums, tiles, *near[1:])
    sums, far_low, far_high = lax.optimization_barrier((sums, far_low, far_high))
    partner_far_low = send(far_low, across)
    partner_far_high = send(far_high, across)
    other = {1: prepare(t_other)}
    sums = add(sums, other, *near)
    both = {**tiles, **other}
    sums = add(sums, both, ((0, 4, 0), far_low), ((middle, 4, 0), far_high))
    sums = add(sums, both, ((0, -2, 1), partner_below), ((0, 2, 1), partner_above))
    sums = add(sums, both, ((0, 4, 1), partner_far_low), ((middle, 4, 1), partner_far_high))

    sums = sums[0] + lax.ppermute(sums[1], "layer", [(0, 1), (1, 0)])
    sums = lax.all_to_all(sums, "row", 0, 0, tiled=True, axis_index_groups=ranks)
    return jnp.sum(sums, axis=0)


def solution(mesh):
    return jax.shard_map(
        on_device,
        mesh=mesh,
        in_specs=(
            P("col", ("row", "layer")),
            P("col", "layer", "row", None, None),
            P("col", "layer", "row", None),
        ),
        out_specs=P("col", ("row", "layer")),
        check_vma=False,
    )
```

```python
import jax
import jax.numpy as jnp
from jax import lax
from jax.experimental import pallas as pl
from jax.experimental.pallas import tpu as pltpu
from jax.sharding import PartitionSpec as P

TILE = 64
AB_DEV = 128
LANES = 128
GROUP = 2
HALF = TILE // 2
VMEM = pl.BlockSpec(memory_space=pltpu.VMEM)
SMEM = pl.BlockSpec(memory_space=pltpu.SMEM)


def split_rows(x):
    hi = x.astype(jnp.bfloat16)
    return hi, (x - hi.astype(jnp.float32)).astype(jnp.bfloat16)


def pack_kernel(spots, lists, out):
    held, slots = spots.shape
    cols = out.shape[0] // held
    pair = slots // cols
    rows = pair * HALF
    lane = lax.broadcasted_iota(jnp.int32, (8, LANES), 1)
    for b in range(held):
        row = jnp.zeros((8, LANES), jnp.float32)
        for s in range(slots):
            row = jnp.where(lane == s, spots[b, s].astype(jnp.float32), row)
        for c in range(cols):
            for p in range(pair):
                s = c * pair + p
                out[b * cols + c, p * HALF : (p + 1) * HALF] = lists[b, s // 8, pl.ds(s % 8, HALF, stride=8), :]
            out[b * cols + c, rows:] = row


def pack(v_tiles, v_where, cols):
    held, slots = v_tiles.shape[0], v_tiles.shape[3]
    lists = v_tiles.reshape(held, slots // 8, 8, HALF, LANES).transpose(0, 1, 3, 2, 4)
    lists = lists.reshape(held, slots // 8, HALF * 8, LANES)
    return pl.pallas_call(
        pack_kernel,
        out_shape=jax.ShapeDtypeStruct((held * cols, slots // cols * HALF + 8, LANES), jnp.float32),
        in_specs=[SMEM, VMEM],
        out_specs=VMEM,
        compiler_params=pltpu.CompilerParams(vmem_limit_bytes=14 * 2**20),
        cost_estimate=pl.CostEstimate(flops=0, bytes_accessed=2**20, transcendentals=0),
    )(v_where.reshape(held, slots), lists)


def prepare_kernel(*refs):
    *halves, t_tiles = refs
    row = lax.broadcasted_iota(jnp.int32, (LANES, 2 * LANES), 0)
    col = lax.broadcasted_iota(jnp.int32, (LANES, 2 * LANES), 1)
    source = (col // LANES) * TILE + 2 * (col % HALF) + (col % TILE) // HALF
    pick = (row == source).astype(jnp.bfloat16)
    for at in range(halves[0].shape[1] // LANES):
        split = [split_rows(half[:, at * LANES : (at + 1) * LANES]) for half in halves]
        rows = jnp.concatenate([hi for hi, _ in split] + [lo for _, lo in split], axis=0)
        both = jnp.dot(rows, pick, preferred_element_type=jnp.float32).astype(jnp.bfloat16)
        t_tiles[2 * at] = both[:, :LANES]
        t_tiles[2 * at + 1] = both[:, LANES:]


def prepare(*halves):
    ij, cd = sum(half.shape[0] for half in halves), halves[0].shape[1]
    return pl.pallas_call(
        prepare_kernel,
        out_shape=jax.ShapeDtypeStruct((cd // TILE, 2 * ij, LANES), jnp.bfloat16),
        in_specs=[VMEM] * len(halves),
        out_specs=VMEM,
        compiler_params=pltpu.CompilerParams(vmem_limit_bytes=14 * 2**20),
        cost_estimate=pl.CostEstimate(flops=2 * 2 * ij * cd * 2 * LANES, bytes_accessed=3 * 2**20, transcendentals=0),
    )(*halves)


def slot_rows(v, spot):
    lane_half = lax.broadcasted_iota(jnp.int32, (HALF, LANES), 1) // TILE
    safe = jnp.maximum(spot, 0)
    ab_half = safe & 1
    ab_pair = (safe >> 1) & 1
    swapped = pltpu.roll(v, TILE, 1)
    upper = ab_half == 1
    keep = (lane_half == ab_half) & (spot >= 0)
    hi_e, lo_e = split_rows(jnp.where(keep, jnp.where(upper, swapped, v), 0.0))
    hi_o, lo_o = split_rows(jnp.where(keep, jnp.where(upper, v, swapped), 0.0))
    rows = jnp.concatenate([hi_e, hi_o, lo_e, lo_o], axis=0)
    none = jnp.zeros_like(rows)
    return jnp.concatenate([jnp.where(ab_pair == 0, rows, none), jnp.where(ab_pair == 1, rows, none)], axis=1)


def contract_kernel(sources, offsets, fresh, pair, group, *refs):
    count, blocks_held = len(sources), len(offsets)
    place, spots = refs[:2]
    t_tiles = refs[2 : 2 + blocks_held]
    shares = refs[2 + blocks_held : 2 + blocks_held + count]
    rest = refs[2 + blocks_held + count :]
    sums = None if fresh else rest[0]
    out = rest[-1]
    layer = place[1]
    blocks, ij = out.shape[1:3]
    rows = pair * HALF
    cols = spots.shape[1] // pair
    columns = [((place[0] + shift) & (cols - 1)) ^ flip for _, shift, flip in sources]
    members = [place[2] ^ offset for offset in offsets]
    for block in range(blocks):
        used = [
            n for n in range(count)
            if sources[n][0] <= block < sources[n][0] + shares[n].shape[0] // (group * rows)
        ]
        total = None
        for n in used:
            for held in range(blocks_held):
                first = pl.multiple_of(((block - sources[n][0]) * group + members[held]) * rows, rows)
                left, right = [], []
                for p in range(pair):
                    spot = spots[block * group + members[held], columns[n] * pair + p]
                    left.append(t_tiles[held][jnp.maximum(spot, 0) >> 2])
                    right.append(slot_rows(shares[n][pl.ds(first + p * HALF, HALF), :], spot))
                part = jnp.dot(
                    jnp.concatenate(left, axis=1),
                    jnp.concatenate(right, axis=0),
                    preferred_element_type=jnp.float32,
                )
                total = part if total is None else total + part
        total = total[:ij] + total[ij:]
        mine = total[:, :LANES]
        other = total[:, LANES:]
        to = place[3] ^ block
        if sums is not None:
            mine = mine + sums[layer, to]
            other = other + sums[1 - layer, to]
        out[layer, to] = mine
        out[1 - layer, to] = other


def contract(sums, place, spots, held, shares, pair):
    group = GROUP
    blocks = spots.shape[0] // group
    ij = next(iter(held.values())).shape[1] // 2
    sources = tuple(source for source, _ in shares)
    offsets = tuple(held)
    given = [place, spots, *held.values(), *(share for _, share in shares)]
    specs = [SMEM, SMEM] + [VMEM] * (len(given) - 2)
    if sums is not None:
        given.append(sums)
        specs.append(VMEM)

    def kernel(*refs):
        contract_kernel(sources, offsets, sums is None, pair, group, *refs)

    return pl.pallas_call(
        kernel,
        out_shape=jax.ShapeDtypeStruct((2, blocks, ij, LANES), jnp.float32),
        in_specs=specs,
        out_specs=VMEM,
        input_output_aliases={} if sums is None else {len(given) - 1: 0},
        compiler_params=pltpu.CompilerParams(vmem_limit_bytes=14 * 2**20),
        cost_estimate=pl.CostEstimate(
            flops=2**12,
            bytes_accessed=2**10,
            transcendentals=0,
        ),
    )(*given)


def sort_kernel(place, parts, *chunks):
    cols = parts.shape[0] // 2
    rows = parts.shape[1] - 8
    for k in range(len(chunks)):
        first = ((place[3] >> 1) ^ k) * GROUP
        at = lax.broadcasted_iota(jnp.int32, (8, LANES), 0)
        spots = jnp.zeros((8, LANES), jnp.float32)
        for x in range(2):
            for e in range(GROUP):
                n, source = x * GROUP + e, x * cols + first + e
                chunks[k][n * rows : (n + 1) * rows] = parts[source, :rows]
                spots = jnp.where(at == n, parts[source, rows:], spots)
        chunks[k][2 * GROUP * rows :] = spots


def sort(place, parts, count):
    rows = parts.shape[1] - 8
    return pl.pallas_call(
        sort_kernel,
        out_shape=[jax.ShapeDtypeStruct((2 * GROUP * rows + 8, LANES), jnp.float32)] * count,
        in_specs=[SMEM, VMEM],
        out_specs=[VMEM] * count,
        compiler_params=pltpu.CompilerParams(vmem_limit_bytes=14 * 2**20),
        cost_estimate=pl.CostEstimate(flops=0, bytes_accessed=2**16, transcendentals=0),
    )(place, parts)


def join_kernel(*refs):
    *chunks, low, high, spots = refs
    half = len(chunks) // 2
    for k, chunk in enumerate(chunks):
        size = chunk.shape[0] - 8
        own, at = (low, high)[k // half], k % half * size
        own[at : at + size] = chunk[:size]
        spots[k] = chunk[size:].astype(jnp.int32)


def join(chunks):
    size = chunks[0].shape[0] - 8
    return pl.pallas_call(
        join_kernel,
        out_shape=[
            jax.ShapeDtypeStruct((len(chunks) // 2 * size, LANES), jnp.float32),
            jax.ShapeDtypeStruct((len(chunks) // 2 * size, LANES), jnp.float32),
            jax.ShapeDtypeStruct((len(chunks), 8, LANES), jnp.int32),
        ],
        in_specs=[VMEM] * len(chunks),
        out_specs=[VMEM] * 3,
        compiler_params=pltpu.CompilerParams(vmem_limit_bytes=14 * 2**20),
        cost_estimate=pl.CostEstimate(flops=0, bytes_accessed=2**16, transcendentals=0),
    )(*chunks)


def on_device(t_amps, v_tiles, v_where):
    cols = lax.axis_size("col")
    rows_axis = lax.axis_size("row")
    held, slots = v_tiles.shape[0], v_tiles.shape[3]
    pair = slots // cols
    rows = pair * HALF
    blocks = rows_axis // GROUP
    ranks = [
        [2 * (GROUP * m + (m.bit_count() + odd) % 2) + x for m in range(blocks // 2) for x in range(2)]
        for odd in range(2)
    ]
    row = lax.axis_index("row")
    place = jnp.stack(
        [lax.axis_index("col"), lax.axis_index("layer"), row // 2 % GROUP, row // (2 * GROUP) * 2]
    )

    def send(share, to, axis="col", size=cols):
        return lax.ppermute(share, axis, [(i, to(i)) for i in range(size)])

    def send_t(t_block):
        return send(t_block, lambda i: i ^ 2, "row", rows_axis)

    planes = [
        [(2 * z + x) * cols + c for x in range(2) for c in range(cols)] for z in range(rows_axis // 2)
    ]
    t_other = send_t(t_amps)
    parts = pack(v_tiles, v_where, cols)
    parts = lax.all_to_all(parts, ("row", "col"), 0, 0, tiled=True, axis_index_groups=planes)
    parts, t_other = lax.optimization_barrier((parts, t_other))
    chunks = sort(place, parts, blocks // 2)

    def send_m(chunk, k):
        return send(chunk, lambda i: i ^ (2 * GROUP * k) ^ (2 * (k.bit_count() % 2)), "row", rows_axis)

    low, high, spots = join([chunks[0]] + [send_m(chunks[k], k) for k in range(1, blocks // 2)])
    spots = spots[:, : 2 * GROUP, :slots].reshape(blocks * GROUP, slots)

    def up(i):
        return (i + 2) % cols

    def down(i):
        return (i - 2) % cols

    def across(i):
        return i ^ 1

    def add(sums, held, *shares):
        return contract(sums, place, spots, held, shares, pair)

    middle = blocks // 2

    def halves(shift, flip, low, high):
        return [((0, shift, flip), low), ((middle, shift, flip), high)]

    below_low, above_high = send(low, up), send(high, down)
    partner_low = send(low, across)
    below_high, above_low = send(high, up), send(low, down)
    partner_high = send(high, across)
    tiles = {0: prepare(t_amps), 1: prepare(t_other)}
    sums = add(None, tiles, *halves(0, 0, low, high))
    sums, below_low, above_high = lax.optimization_barrier((sums, below_low, above_high))
    far_low, far_high = send(below_low, up), send(above_high, down)
    partner_below_low, partner_above_low = send(partner_low, up), send(partner_low, down)
    partner_below_high, partner_above_high = send(partner_high, up), send(partner_high, down)
    sums = add(
        sums,
        tiles,
        *halves(0, 1, partner_low, partner_high),
        *halves(-2, 0, below_low, below_high),
        *halves(2, 0, above_low, above_high),
    )
    sums, far_low, far_high = lax.optimization_barrier((sums, far_low, far_high))
    partner_far_low, partner_far_high = send(far_low, across), send(far_high, across)
    sums = add(
        sums,
        tiles,
        *halves(4, 0, far_low, far_high),
        ((0, -2, 1), partner_below_low),
        ((0, 2, 1), partner_above_low),
    )
    sums = add(
        sums,
        tiles,
        ((middle, -2, 1), partner_below_high),
        ((middle, 2, 1), partner_above_high),
        *halves(4, 1, partner_far_low, partner_far_high),
    )
    sums = sums[0] + lax.ppermute(sums[1], "layer", [(0, 1), (1, 0)])
    sums = lax.all_to_all(sums, "row", 0, 0, tiled=True, axis_index_groups=ranks)
    return jnp.sum(sums, axis=0)


def solution(mesh):
    return jax.shard_map(
        on_device,
        mesh=mesh,
        in_specs=(
            P("col", ("row", "layer")),
            P("col", "layer", "row", None, None),
            P("col", "layer", "row", None),
        ),
        out_specs=P("col", ("row", "layer")),
        check_vma=False,
    )
```

```python
import jax
import jax.numpy as jnp
from jax import lax
from jax.experimental import pallas as pl
from jax.experimental.pallas import tpu as pltpu
from jax.sharding import PartitionSpec as P

TILE = 64
AB_DEV = 128
LANES = 128
GROUP = 2
HALF = TILE // 2
VMEM = pl.BlockSpec(memory_space=pltpu.VMEM)
SMEM = pl.BlockSpec(memory_space=pltpu.SMEM)


def split_rows(x):
    hi = x.astype(jnp.bfloat16)
    return hi, (x - hi.astype(jnp.float32)).astype(jnp.bfloat16)


def pack_kernel(spots, lists, out):
    held, slots = spots.shape
    cols = out.shape[0] // held
    pair = slots // cols
    rows = pair * HALF
    lane = lax.broadcasted_iota(jnp.int32, (8, LANES), 1)
    for b in range(held):
        row = jnp.zeros((8, LANES), jnp.float32)
        for s in range(slots):
            row = jnp.where(lane == s, spots[b, s].astype(jnp.float32), row)
        for c in range(cols):
            for p in range(pair):
                s = c * pair + p
                out[b * cols + c, p * HALF : (p + 1) * HALF] = lists[b, s // 8, pl.ds(s % 8, HALF, stride=8), :]
            out[b * cols + c, rows:] = row


def pack(v_tiles, v_where, cols):
    held, slots = v_tiles.shape[0], v_tiles.shape[3]
    lists = v_tiles.reshape(held, slots // 8, 8, HALF, LANES).transpose(0, 1, 3, 2, 4)
    lists = lists.reshape(held, slots // 8, HALF * 8, LANES)
    return pl.pallas_call(
        pack_kernel,
        out_shape=jax.ShapeDtypeStruct((held * cols, slots // cols * HALF + 8, LANES), jnp.float32),
        in_specs=[SMEM, VMEM],
        out_specs=VMEM,
        compiler_params=pltpu.CompilerParams(vmem_limit_bytes=14 * 2**20),
        cost_estimate=pl.CostEstimate(flops=0, bytes_accessed=2**20, transcendentals=0),
    )(v_where.reshape(held, slots), lists)


def prepare_kernel(*refs):
    *halves, t_tiles = refs
    row = lax.broadcasted_iota(jnp.int32, (LANES, 2 * LANES), 0)
    col = lax.broadcasted_iota(jnp.int32, (LANES, 2 * LANES), 1)
    source = (col // LANES) * TILE + 2 * (col % HALF) + (col % TILE) // HALF
    pick = (row == source).astype(jnp.bfloat16)
    for at in range(halves[0].shape[1] // LANES):
        split = [split_rows(half[:, at * LANES : (at + 1) * LANES]) for half in halves]
        rows = jnp.concatenate([hi for hi, _ in split] + [lo for _, lo in split], axis=0)
        both = jnp.dot(rows, pick, preferred_element_type=jnp.float32).astype(jnp.bfloat16)
        t_tiles[2 * at] = both[:, :LANES]
        t_tiles[2 * at + 1] = both[:, LANES:]


def prepare(*halves):
    ij, cd = sum(half.shape[0] for half in halves), halves[0].shape[1]
    return pl.pallas_call(
        prepare_kernel,
        out_shape=jax.ShapeDtypeStruct((cd // TILE, 2 * ij, LANES), jnp.bfloat16),
        in_specs=[VMEM] * len(halves),
        out_specs=VMEM,
        compiler_params=pltpu.CompilerParams(vmem_limit_bytes=14 * 2**20),
        cost_estimate=pl.CostEstimate(flops=2 * 2 * ij * cd * 2 * LANES, bytes_accessed=3 * 2**20, transcendentals=0),
    )(*halves)


def slot_rows(v, spot):
    lane_half = lax.broadcasted_iota(jnp.int32, (HALF, LANES), 1) // TILE
    safe = jnp.maximum(spot, 0)
    ab_half = safe & 1
    ab_pair = (safe >> 1) & 1
    swapped = pltpu.roll(v, TILE, 1)
    upper = ab_half == 1
    keep = (lane_half == ab_half) & (spot >= 0)
    hi_e, lo_e = split_rows(jnp.where(keep, jnp.where(upper, swapped, v), 0.0))
    hi_o, lo_o = split_rows(jnp.where(keep, jnp.where(upper, v, swapped), 0.0))
    rows = jnp.concatenate([hi_e, hi_o, lo_e, lo_o], axis=0)
    none = jnp.zeros_like(rows)
    return jnp.concatenate([jnp.where(ab_pair == 0, rows, none), jnp.where(ab_pair == 1, rows, none)], axis=1)


def contract_kernel(sources, offsets, fresh, pair, group, *refs):
    count, blocks_held = len(sources), len(offsets)
    place, spots = refs[:2]
    t_tiles = refs[2 : 2 + blocks_held]
    shares = refs[2 + blocks_held : 2 + blocks_held + count]
    rest = refs[2 + blocks_held + count :]
    sums = None if fresh else rest[0]
    out = rest[-1]
    layer = place[1]
    blocks, ij = out.shape[1:3]
    rows = pair * HALF
    cols = spots.shape[1] // pair
    columns = [((place[0] + shift) & (cols - 1)) ^ flip for _, shift, flip in sources]
    members = [place[2] ^ offset for offset in offsets]
    for block in range(blocks):
        used = [
            n for n in range(count)
            if sources[n][0] <= block < sources[n][0] + shares[n].shape[0] // (group * rows)
        ]
        total = None
        for n in used:
            for held in range(blocks_held):
                first = pl.multiple_of(((block - sources[n][0]) * group + members[held]) * rows, rows)
                left, right = [], []
                for p in range(pair):
                    spot = spots[block * group + members[held], columns[n] * pair + p]
                    left.append(t_tiles[held][jnp.maximum(spot, 0) >> 2])
                    right.append(slot_rows(shares[n][pl.ds(first + p * HALF, HALF), :], spot))
                part = jnp.dot(
                    jnp.concatenate(left, axis=1),
                    jnp.concatenate(right, axis=0),
                    preferred_element_type=jnp.float32,
                )
                total = part if total is None else total + part
        total = total[:ij] + total[ij:]
        mine = total[:, :LANES]
        other = total[:, LANES:]
        to = place[3] ^ block
        if sums is not None:
            mine = mine + sums[layer, to]
            other = other + sums[1 - layer, to]
        out[layer, to] = mine
        out[1 - layer, to] = other


def contract(sums, place, spots, held, shares, pair):
    group = GROUP
    blocks = spots.shape[0] // group
    ij = next(iter(held.values())).shape[1] // 2
    sources = tuple(source for source, _ in shares)
    offsets = tuple(held)
    given = [place, spots, *held.values(), *(share for _, share in shares)]
    specs = [SMEM, SMEM] + [VMEM] * (len(given) - 2)
    if sums is not None:
        given.append(sums)
        specs.append(VMEM)

    def kernel(*refs):
        contract_kernel(sources, offsets, sums is None, pair, group, *refs)

    return pl.pallas_call(
        kernel,
        out_shape=jax.ShapeDtypeStruct((2, blocks, ij, LANES), jnp.float32),
        in_specs=specs,
        out_specs=VMEM,
        input_output_aliases={} if sums is None else {len(given) - 1: 0},
        compiler_params=pltpu.CompilerParams(vmem_limit_bytes=14 * 2**20),
        cost_estimate=pl.CostEstimate(
            flops=2**12,
            bytes_accessed=2**10,
            transcendentals=0,
        ),
    )(*given)


def sort_kernel(place, parts, *chunks):
    cols = parts.shape[0] // 2
    rows = parts.shape[1] - 8
    for k in range(len(chunks)):
        first = ((place[3] >> 1) ^ k) * GROUP
        at = lax.broadcasted_iota(jnp.int32, (8, LANES), 0)
        spots = jnp.zeros((8, LANES), jnp.float32)
        for x in range(2):
            for e in range(GROUP):
                n, source = x * GROUP + e, x * cols + first + e
                chunks[k][n * rows : (n + 1) * rows] = parts[source, :rows]
                spots = jnp.where(at == n, parts[source, rows:], spots)
        chunks[k][2 * GROUP * rows :] = spots


def sort(place, parts, count):
    rows = parts.shape[1] - 8
    return pl.pallas_call(
        sort_kernel,
        out_shape=[jax.ShapeDtypeStruct((2 * GROUP * rows + 8, LANES), jnp.float32)] * count,
        in_specs=[SMEM, VMEM],
        out_specs=[VMEM] * count,
        compiler_params=pltpu.CompilerParams(vmem_limit_bytes=14 * 2**20),
        cost_estimate=pl.CostEstimate(flops=0, bytes_accessed=2**16, transcendentals=0),
    )(place, parts)


def join_kernel(*refs):
    *chunks, own, spots = refs
    for k, chunk in enumerate(chunks):
        size = chunk.shape[0] - 8
        own[k * size : (k + 1) * size] = chunk[:size]
        spots[k] = chunk[size:].astype(jnp.int32)


def join(chunks):
    size = chunks[0].shape[0] - 8
    return pl.pallas_call(
        join_kernel,
        out_shape=[
            jax.ShapeDtypeStruct((len(chunks) * size, LANES), jnp.float32),
            jax.ShapeDtypeStruct((len(chunks), 8, LANES), jnp.int32),
        ],
        in_specs=[VMEM] * len(chunks),
        out_specs=[VMEM] * 2,
        compiler_params=pltpu.CompilerParams(vmem_limit_bytes=14 * 2**20),
        cost_estimate=pl.CostEstimate(flops=0, bytes_accessed=2**16, transcendentals=0),
    )(*chunks)


def on_device(t_amps, v_tiles, v_where):
    cols = lax.axis_size("col")
    rows_axis = lax.axis_size("row")
    held, slots = v_tiles.shape[0], v_tiles.shape[3]
    pair = slots // cols
    rows = pair * HALF
    blocks = rows_axis // GROUP
    ranks = [
        [2 * (GROUP * m + (m.bit_count() + odd) % 2) + x for m in range(blocks // 2) for x in range(2)]
        for odd in range(2)
    ]
    row = lax.axis_index("row")
    place = jnp.stack(
        [lax.axis_index("col"), lax.axis_index("layer"), row // 2 % GROUP, row // (2 * GROUP) * 2]
    )

    def send(share, to, axis="col", size=cols):
        return lax.ppermute(share, axis, [(i, to(i)) for i in range(size)])

    def send_t(t_block):
        return send(t_block, lambda i: i ^ 2, "row", rows_axis)

    planes = [
        [(2 * z + x) * cols + c for x in range(2) for c in range(cols)] for z in range(rows_axis // 2)
    ]
    parts = pack(v_tiles, v_where, cols)
    parts = lax.all_to_all(parts, ("row", "col"), 0, 0, tiled=True, axis_index_groups=planes)
    chunks = sort(place, parts, blocks // 2)

    def send_m(chunk, k):
        return send(chunk, lambda i: i ^ (2 * GROUP * k) ^ (2 * (k.bit_count() % 2)), "row", rows_axis)

    own, spots = join([chunks[0]] + [send_m(chunks[k], k) for k in range(1, blocks // 2)])
    spots = spots[:, : 2 * GROUP, :slots].reshape(blocks * GROUP, slots)

    def up(i):
        return (i + 2) % cols

    def down(i):
        return (i - 2) % cols

    def across(i):
        return i ^ 1

    def add(sums, held, *shares):
        return contract(sums, place, spots, held, shares, pair)

    half, middle = own.shape[0] // 2, blocks // 2
    partner = send(own, across)
    below = send(own, up)
    above = send(own, down)
    tiles = {0: prepare(t_amps)}
    sums = add(None, tiles, ((0, 0, 0), own))
    sums, t_other = lax.optimization_barrier((sums, t_amps))
    t_other = send_t(t_other)
    sums, partner, below, above = lax.optimization_barrier((sums, partner, below, above))
    far_low = send(below[:half], up)
    far_high = send(above[half:], down)
    partner_below = send(partner, up)
    partner_above = send(partner, down)
    near = [((0, 0, 0), own), ((0, 0, 1), partner), ((0, -2, 0), below), ((0, 2, 0), above)]
    sums = add(sums, tiles, *near[1:])
    sums, far_low, far_high = lax.optimization_barrier((sums, far_low, far_high))
    partner_far_low = send(far_low, across)
    partner_far_high = send(far_high, across)
    other = {1: prepare(t_other)}
    sums = add(sums, other, *near)
    both = {**tiles, **other}
    sums = add(sums, both, ((0, 4, 0), far_low), ((middle, 4, 0), far_high))
    sums = add(sums, both, ((0, -2, 1), partner_below), ((0, 2, 1), partner_above))
    sums = add(sums, both, ((0, 4, 1), partner_far_low), ((middle, 4, 1), partner_far_high))

    sums = sums[0] + lax.ppermute(sums[1], "layer", [(0, 1), (1, 0)])
    sums = lax.all_to_all(sums, "row", 0, 0, tiled=True, axis_index_groups=ranks)
    return jnp.sum(sums, axis=0)


def solution(mesh):
    return jax.shard_map(
        on_device,
        mesh=mesh,
        in_specs=(
            P("col", ("row", "layer")),
            P("col", "layer", "row", None, None),
            P("col", "layer", "row", None),
        ),
        out_specs=P("col", ("row", "layer")),
        check_vma=False,
    )
```

```python
import jax
import jax.numpy as jnp
from jax import lax
from jax.experimental import pallas as pl
from jax.experimental.pallas import tpu as pltpu
from jax.sharding import PartitionSpec as P

TILE = 64
AB_DEV = 128
LANES = 128
GROUP = 2
HALF = TILE // 2
VMEM = pl.BlockSpec(memory_space=pltpu.VMEM)
SMEM = pl.BlockSpec(memory_space=pltpu.SMEM)


def split_rows(x):
    hi = x.astype(jnp.bfloat16)
    return hi, (x - hi.astype(jnp.float32)).astype(jnp.bfloat16)


def pack_kernel(spots, lists, out):
    held, slots = spots.shape
    cols = out.shape[0] // held
    pair = slots // cols
    rows = pair * HALF
    lane = lax.broadcasted_iota(jnp.int32, (8, LANES), 1)
    for b in range(held):
        row = jnp.zeros((8, LANES), jnp.float32)
        for s in range(slots):
            row = jnp.where(lane == s, spots[b, s].astype(jnp.float32), row)
        for c in range(cols):
            for p in range(pair):
                s = c * pair + p
                out[b * cols + c, p * HALF : (p + 1) * HALF] = lists[b, s // 8, pl.ds(s % 8, HALF, stride=8), :]
            out[b * cols + c, rows:] = row


def pack(v_tiles, v_where, cols):
    held, slots = v_tiles.shape[0], v_tiles.shape[3]
    lists = v_tiles.reshape(held, slots // 8, 8, HALF, LANES).transpose(0, 1, 3, 2, 4)
    lists = lists.reshape(held, slots // 8, HALF * 8, LANES)
    return pl.pallas_call(
        pack_kernel,
        out_shape=jax.ShapeDtypeStruct((held * cols, slots // cols * HALF + 8, LANES), jnp.float32),
        in_specs=[SMEM, VMEM],
        out_specs=VMEM,
        compiler_params=pltpu.CompilerParams(vmem_limit_bytes=14 * 2**20),
        cost_estimate=pl.CostEstimate(flops=0, bytes_accessed=2**20, transcendentals=0),
    )(v_where.reshape(held, slots), lists)


def prepare_kernel(*refs):
    *halves, t_tiles = refs
    row = lax.broadcasted_iota(jnp.int32, (LANES, 2 * LANES), 0)
    col = lax.broadcasted_iota(jnp.int32, (LANES, 2 * LANES), 1)
    source = (col // LANES) * TILE + 2 * (col % HALF) + (col % TILE) // HALF
    pick = (row == source).astype(jnp.bfloat16)
    for at in range(halves[0].shape[1] // LANES):
        split = [split_rows(half[:, at * LANES : (at + 1) * LANES]) for half in halves]
        rows = jnp.concatenate([hi for hi, _ in split] + [lo for _, lo in split], axis=0)
        both = jnp.dot(rows, pick, preferred_element_type=jnp.float32).astype(jnp.bfloat16)
        t_tiles[2 * at] = both[:, :LANES]
        t_tiles[2 * at + 1] = both[:, LANES:]


def prepare(*halves):
    ij, cd = sum(half.shape[0] for half in halves), halves[0].shape[1]
    return pl.pallas_call(
        prepare_kernel,
        out_shape=jax.ShapeDtypeStruct((cd // TILE, 2 * ij, LANES), jnp.bfloat16),
        in_specs=[VMEM] * len(halves),
        out_specs=VMEM,
        compiler_params=pltpu.CompilerParams(vmem_limit_bytes=14 * 2**20),
        cost_estimate=pl.CostEstimate(flops=2 * 2 * ij * cd * 2 * LANES, bytes_accessed=3 * 2**20, transcendentals=0),
    )(*halves)


def slot_rows(v, spot):
    lane_half = lax.broadcasted_iota(jnp.int32, (HALF, LANES), 1) // TILE
    safe = jnp.maximum(spot, 0)
    ab_half = safe & 1
    ab_pair = (safe >> 1) & 1
    swapped = pltpu.roll(v, TILE, 1)
    upper = ab_half == 1
    keep = (lane_half == ab_half) & (spot >= 0)
    hi_e, lo_e = split_rows(jnp.where(keep, jnp.where(upper, swapped, v), 0.0))
    hi_o, lo_o = split_rows(jnp.where(keep, jnp.where(upper, v, swapped), 0.0))
    rows = jnp.concatenate([hi_e, hi_o, lo_e, lo_o], axis=0)
    none = jnp.zeros_like(rows)
    return jnp.concatenate([jnp.where(ab_pair == 0, rows, none), jnp.where(ab_pair == 1, rows, none)], axis=1)


def contract_kernel(sources, offsets, fresh, pair, group, *refs):
    count, blocks_held = len(sources), len(offsets)
    place, spots = refs[:2]
    t_tiles = refs[2 : 2 + blocks_held]
    shares = refs[2 + blocks_held : 2 + blocks_held + count]
    rest = refs[2 + blocks_held + count :]
    sums = None if fresh else rest[0]
    out = rest[-1]
    layer = place[1]
    blocks, ij = out.shape[1:3]
    rows = pair * HALF
    cols = spots.shape[1] // pair
    columns = [((place[0] + shift) & (cols - 1)) ^ flip for _, shift, flip in sources]
    members = [place[2] ^ offset for offset in offsets]
    for block in range(blocks):
        used = [
            n for n in range(count)
            if sources[n][0] <= block < sources[n][0] + shares[n].shape[0] // (group * rows)
        ]
        total = None
        for n in used:
            for held in range(blocks_held):
                first = pl.multiple_of(((block - sources[n][0]) * group + members[held]) * rows, rows)
                left, right = [], []
                for p in range(pair):
                    spot = spots[block * group + members[held], columns[n] * pair + p]
                    left.append(t_tiles[held][jnp.maximum(spot, 0) >> 2])
                    right.append(slot_rows(shares[n][pl.ds(first + p * HALF, HALF), :], spot))
                part = jnp.dot(
                    jnp.concatenate(left, axis=1),
                    jnp.concatenate(right, axis=0),
                    preferred_element_type=jnp.float32,
                )
                total = part if total is None else total + part
        total = total[:ij] + total[ij:]
        mine = total[:, :LANES]
        other = total[:, LANES:]
        to = place[3] ^ block
        if sums is not None:
            mine = mine + sums[layer, to]
            other = other + sums[1 - layer, to]
        out[layer, to] = mine
        out[1 - layer, to] = other


def contract(sums, place, spots, held, shares, pair):
    group = GROUP
    blocks = spots.shape[0] // group
    ij = next(iter(held.values())).shape[1] // 2
    sources = tuple(source for source, _ in shares)
    offsets = tuple(held)
    given = [place, spots, *held.values(), *(share for _, share in shares)]
    specs = [SMEM, SMEM] + [VMEM] * (len(given) - 2)
    if sums is not None:
        given.append(sums)
        specs.append(VMEM)

    def kernel(*refs):
        contract_kernel(sources, offsets, sums is None, pair, group, *refs)

    return pl.pallas_call(
        kernel,
        out_shape=jax.ShapeDtypeStruct((2, blocks, ij, LANES), jnp.float32),
        in_specs=specs,
        out_specs=VMEM,
        input_output_aliases={} if sums is None else {len(given) - 1: 0},
        compiler_params=pltpu.CompilerParams(vmem_limit_bytes=14 * 2**20),
        cost_estimate=pl.CostEstimate(
            flops=2**12,
            bytes_accessed=2**10,
            transcendentals=0,
        ),
    )(*given)


def sort_kernel(place, parts, *chunks):
    cols = parts.shape[0] // 2
    rows = parts.shape[1] - 8
    for k in range(len(chunks)):
        first = ((place[3] >> 1) ^ k) * GROUP
        at = lax.broadcasted_iota(jnp.int32, (8, LANES), 0)
        spots = jnp.zeros((8, LANES), jnp.float32)
        for x in range(2):
            for e in range(GROUP):
                n, source = x * GROUP + e, x * cols + first + e
                chunks[k][n * rows : (n + 1) * rows] = parts[source, :rows]
                spots = jnp.where(at == n, parts[source, rows:], spots)
        chunks[k][2 * GROUP * rows :] = spots


def sort(place, parts, count):
    rows = parts.shape[1] - 8
    return pl.pallas_call(
        sort_kernel,
        out_shape=[jax.ShapeDtypeStruct((2 * GROUP * rows + 8, LANES), jnp.float32)] * count,
        in_specs=[SMEM, VMEM],
        out_specs=[VMEM] * count,
        compiler_params=pltpu.CompilerParams(vmem_limit_bytes=14 * 2**20),
        cost_estimate=pl.CostEstimate(flops=0, bytes_accessed=2**16, transcendentals=0),
    )(place, parts)


def join_kernel(*refs):
    *chunks, own, spots = refs
    for k, chunk in enumerate(chunks):
        size = chunk.shape[0] - 8
        own[k * size : (k + 1) * size] = chunk[:size]
        spots[k] = chunk[size:].astype(jnp.int32)


def join(chunks):
    size = chunks[0].shape[0] - 8
    return pl.pallas_call(
        join_kernel,
        out_shape=[
            jax.ShapeDtypeStruct((len(chunks) * size, LANES), jnp.float32),
            jax.ShapeDtypeStruct((len(chunks), 8, LANES), jnp.int32),
        ],
        in_specs=[VMEM] * len(chunks),
        out_specs=[VMEM] * 2,
        compiler_params=pltpu.CompilerParams(vmem_limit_bytes=14 * 2**20),
        cost_estimate=pl.CostEstimate(flops=0, bytes_accessed=2**16, transcendentals=0),
    )(*chunks)


def on_device(t_amps, v_tiles, v_where):
    cols = lax.axis_size("col")
    rows_axis = lax.axis_size("row")
    held, slots = v_tiles.shape[0], v_tiles.shape[3]
    pair = slots // cols
    rows = pair * HALF
    blocks = rows_axis // GROUP
    ranks = [
        [2 * (GROUP * m + (m.bit_count() + odd) % 2) + x for m in range(blocks // 2) for x in range(2)]
        for odd in range(2)
    ]
    row = lax.axis_index("row")
    place = jnp.stack(
        [lax.axis_index("col"), lax.axis_index("layer"), row // 2 % GROUP, row // (2 * GROUP) * 2]
    )

    def send(share, to, axis="col", size=cols):
        return lax.ppermute(share, axis, [(i, to(i)) for i in range(size)])

    def send_t(t_block):
        return send(t_block, lambda i: i ^ 2, "row", rows_axis)

    planes = [
        [(2 * z + x) * cols + c for x in range(2) for c in range(cols)] for z in range(rows_axis // 2)
    ]
    parts = pack(v_tiles, v_where, cols)
    parts = lax.all_to_all(parts, ("row", "col"), 0, 0, tiled=True, axis_index_groups=planes)
    chunks = sort(place, parts, blocks // 2)

    def send_m(chunk, k):
        return send(chunk, lambda i: i ^ (2 * GROUP * k) ^ (2 * (k.bit_count() % 2)), "row", rows_axis)

    own, spots = join([chunks[0]] + [send_m(chunks[k], k) for k in range(1, blocks // 2)])
    spots = spots[:, : 2 * GROUP, :slots].reshape(blocks * GROUP, slots)
    own, t_other, t_own = lax.optimization_barrier((own, t_amps, t_amps))

    def up(i):
        return (i + 2) % cols

    def down(i):
        return (i - 2) % cols

    def across(i):
        return i ^ 1

    def add(sums, held, *shares):
        return contract(sums, place, spots, held, shares, pair)

    half, middle = own.shape[0] // 2, blocks // 2
    partner = send(own, across)
    below = send(own, up)
    above = send(own, down)
    t_other = send_t(t_other)
    tiles = {0: prepare(t_own)}
    sums = add(None, tiles, ((0, 0, 0), own))
    sums, partner, below, above = lax.optimization_barrier((sums, partner, below, above))
    far_low = send(below[:half], up)
    far_high = send(above[half:], down)
    partner_below = send(partner, up)
    partner_above = send(partner, down)
    near = [((0, 0, 0), own), ((0, 0, 1), partner), ((0, -2, 0), below), ((0, 2, 0), above)]
    sums = add(sums, tiles, *near[1:])
    sums, far_low, far_high = lax.optimization_barrier((sums, far_low, far_high))
    partner_far_low = send(far_low, across)
    partner_far_high = send(far_high, across)
    other = {1: prepare(t_other)}
    sums = add(sums, other, *near)
    both = {**tiles, **other}
    sums = add(sums, both, ((0, 4, 0), far_low), ((middle, 4, 0), far_high))
    sums = add(sums, both, ((0, -2, 1), partner_below), ((0, 2, 1), partner_above))
    sums = add(sums, both, ((0, 4, 1), partner_far_low), ((middle, 4, 1), partner_far_high))

    sums = sums[0] + lax.ppermute(sums[1], "layer", [(0, 1), (1, 0)])
    sums = lax.all_to_all(sums, "row", 0, 0, tiled=True, axis_index_groups=ranks)
    return jnp.sum(sums, axis=0)


def solution(mesh):
    return jax.shard_map(
        on_device,
        mesh=mesh,
        in_specs=(
            P("col", ("row", "layer")),
            P("col", "layer", "row", None, None),
            P("col", "layer", "row", None),
        ),
        out_specs=P("col", ("row", "layer")),
        check_vma=False,
    )
```

```python
import jax
import jax.numpy as jnp
from jax import lax
from jax.experimental import pallas as pl
from jax.experimental.pallas import tpu as pltpu
from jax.sharding import PartitionSpec as P

TILE = 64
AB_DEV = 128
LANES = 128
GROUP = 2
HALF = TILE // 2
VMEM = pl.BlockSpec(memory_space=pltpu.VMEM)
SMEM = pl.BlockSpec(memory_space=pltpu.SMEM)
ANYWHERE = pl.BlockSpec(memory_space=pl.ANY)


def split_rows(x):
    hi = x.astype(jnp.bfloat16)
    return hi, (x - hi.astype(jnp.float32)).astype(jnp.bfloat16)


def pack_kernel(spots_in, lists_in, out, spots, lists, arrived):
    copies = [pltpu.make_async_copy(spots_in, spots, arrived.at[0])]
    for b in range(lists.shape[0]):
        copies.append(pltpu.make_async_copy(lists_in.at[b], lists.at[b], arrived.at[1 + b]))
    for copy in copies:
        copy.start()
    copies[0].wait()
    held, slots = spots.shape
    cols = out.shape[0] // held
    pair = slots // cols
    rows = pair * HALF
    lane = lax.broadcasted_iota(jnp.int32, (8, LANES), 1)
    for b in range(held):
        copies[1 + b].wait()
        row = jnp.zeros((8, LANES), jnp.float32)
        for s in range(slots):
            row = jnp.where(lane == s, spots[b, s].astype(jnp.float32), row)
        for c in range(cols):
            for p in range(pair):
                s = c * pair + p
                out[b * cols + c, p * HALF : (p + 1) * HALF] = lists[b, s // 8, pl.ds(s % 8, HALF, stride=8), :]
            out[b * cols + c, rows:] = row


def pack(v_tiles, v_where, cols):
    held, slots = v_tiles.shape[0], v_tiles.shape[3]
    lists = v_tiles.reshape(held, slots // 8, 8, HALF, LANES).transpose(0, 1, 3, 2, 4)
    lists = lists.reshape(held, slots // 8, HALF * 8, LANES)
    return pl.pallas_call(
        pack_kernel,
        out_shape=jax.ShapeDtypeStruct((held * cols, slots // cols * HALF + 8, LANES), jnp.float32),
        in_specs=[ANYWHERE, ANYWHERE],
        out_specs=VMEM,
        scratch_shapes=[
            pltpu.SMEM((held, slots), jnp.int32),
            pltpu.VMEM(lists.shape, jnp.float32),
            pltpu.SemaphoreType.DMA((1 + held,)),
        ],
        compiler_params=pltpu.CompilerParams(vmem_limit_bytes=60 * 2**20),
        cost_estimate=pl.CostEstimate(flops=0, bytes_accessed=2**20, transcendentals=0),
    )(v_where.reshape(held, slots), lists)


def prepare_kernel(*refs):
    *halves, t_tiles = refs
    row = lax.broadcasted_iota(jnp.int32, (LANES, 2 * LANES), 0)
    col = lax.broadcasted_iota(jnp.int32, (LANES, 2 * LANES), 1)
    source = (col // LANES) * TILE + 2 * (col % HALF) + (col % TILE) // HALF
    pick = (row == source).astype(jnp.bfloat16)
    for at in range(halves[0].shape[1] // LANES):
        split = [split_rows(half[:, at * LANES : (at + 1) * LANES]) for half in halves]
        rows = jnp.concatenate([hi for hi, _ in split] + [lo for _, lo in split], axis=0)
        both = jnp.dot(rows, pick, preferred_element_type=jnp.float32).astype(jnp.bfloat16)
        t_tiles[2 * at] = both[:, :LANES]
        t_tiles[2 * at + 1] = both[:, LANES:]


def prepare(*halves):
    ij, cd = sum(half.shape[0] for half in halves), halves[0].shape[1]
    return pl.pallas_call(
        prepare_kernel,
        out_shape=jax.ShapeDtypeStruct((cd // TILE, 2 * ij, LANES), jnp.bfloat16),
        in_specs=[VMEM] * len(halves),
        out_specs=VMEM,
        compiler_params=pltpu.CompilerParams(vmem_limit_bytes=14 * 2**20),
        cost_estimate=pl.CostEstimate(flops=2 * 2 * ij * cd * 2 * LANES, bytes_accessed=3 * 2**20, transcendentals=0),
    )(*halves)


def slot_rows(v, spot):
    lane_half = lax.broadcasted_iota(jnp.int32, (HALF, LANES), 1) // TILE
    safe = jnp.maximum(spot, 0)
    ab_half = safe & 1
    ab_pair = (safe >> 1) & 1
    swapped = pltpu.roll(v, TILE, 1)
    upper = ab_half == 1
    keep = (lane_half == ab_half) & (spot >= 0)
    hi_e, lo_e = split_rows(jnp.where(keep, jnp.where(upper, swapped, v), 0.0))
    hi_o, lo_o = split_rows(jnp.where(keep, jnp.where(upper, v, swapped), 0.0))
    rows = jnp.concatenate([hi_e, hi_o, lo_e, lo_o], axis=0)
    none = jnp.zeros_like(rows)
    return jnp.concatenate([jnp.where(ab_pair == 0, rows, none), jnp.where(ab_pair == 1, rows, none)], axis=1)


def contract_kernel(sources, offsets, fresh, pair, group, *refs):
    count, blocks_held = len(sources), len(offsets)
    place, spots = refs[:2]
    t_tiles = refs[2 : 2 + blocks_held]
    shares = refs[2 + blocks_held : 2 + blocks_held + count]
    rest = refs[2 + blocks_held + count :]
    sums = None if fresh else rest[0]
    out = rest[-1]
    layer = place[1]
    blocks, ij = out.shape[1:3]
    rows = pair * HALF
    cols = spots.shape[1] // pair
    columns = [((place[0] + shift) & (cols - 1)) ^ flip for _, shift, flip in sources]
    members = [place[2] ^ offset for offset in offsets]
    for block in range(blocks):
        used = [
            n for n in range(count)
            if sources[n][0] <= block < sources[n][0] + shares[n].shape[0] // (group * rows)
        ]
        total = None
        for n in used:
            for held in range(blocks_held):
                first = pl.multiple_of(((block - sources[n][0]) * group + members[held]) * rows, rows)
                left, right = [], []
                for p in range(pair):
                    spot = spots[block * group + members[held], columns[n] * pair + p]
                    left.append(t_tiles[held][jnp.maximum(spot, 0) >> 2])
                    right.append(slot_rows(shares[n][pl.ds(first + p * HALF, HALF), :], spot))
                part = jnp.dot(
                    jnp.concatenate(left, axis=1),
                    jnp.concatenate(right, axis=0),
                    preferred_element_type=jnp.float32,
                )
                total = part if total is None else total + part
        total = total[:ij] + total[ij:]
        mine = total[:, :LANES]
        other = total[:, LANES:]
        to = place[3] ^ block
        if sums is not None:
            mine = mine + sums[layer, to]
            other = other + sums[1 - layer, to]
        out[layer, to] = mine
        out[1 - layer, to] = other


def contract(sums, place, spots, held, shares, pair):
    group = GROUP
    blocks = spots.shape[0] // group
    ij = next(iter(held.values())).shape[1] // 2
    sources = tuple(source for source, _ in shares)
    offsets = tuple(held)
    given = [place, spots, *held.values(), *(share for _, share in shares)]
    specs = [SMEM, SMEM] + [VMEM] * (len(given) - 2)
    if sums is not None:
        given.append(sums)
        specs.append(VMEM)

    def kernel(*refs):
        contract_kernel(sources, offsets, sums is None, pair, group, *refs)

    return pl.pallas_call(
        kernel,
        out_shape=jax.ShapeDtypeStruct((2, blocks, ij, LANES), jnp.float32),
        in_specs=specs,
        out_specs=VMEM,
        input_output_aliases={} if sums is None else {len(given) - 1: 0},
        compiler_params=pltpu.CompilerParams(vmem_limit_bytes=14 * 2**20),
        cost_estimate=pl.CostEstimate(
            flops=2**12,
            bytes_accessed=2**10,
            transcendentals=0,
        ),
    )(*given)


def sort_kernel(place, parts, *chunks):
    cols = parts.shape[0] // 2
    rows = parts.shape[1] - 8
    for k in range(len(chunks)):
        first = ((place[3] >> 1) ^ k) * GROUP
        at = lax.broadcasted_iota(jnp.int32, (8, LANES), 0)
        spots = jnp.zeros((8, LANES), jnp.float32)
        for x in range(2):
            for e in range(GROUP):
                n, source = x * GROUP + e, x * cols + first + e
                chunks[k][n * rows : (n + 1) * rows] = parts[source, :rows]
                spots = jnp.where(at == n, parts[source, rows:], spots)
        chunks[k][2 * GROUP * rows :] = spots


def sort(place, parts, count):
    rows = parts.shape[1] - 8
    return pl.pallas_call(
        sort_kernel,
        out_shape=[jax.ShapeDtypeStruct((2 * GROUP * rows + 8, LANES), jnp.float32)] * count,
        in_specs=[SMEM, VMEM],
        out_specs=[VMEM] * count,
        compiler_params=pltpu.CompilerParams(vmem_limit_bytes=14 * 2**20),
        cost_estimate=pl.CostEstimate(flops=0, bytes_accessed=2**16, transcendentals=0),
    )(place, parts)


def join_kernel(*refs):
    *chunks, own, spots = refs
    for k, chunk in enumerate(chunks):
        size = chunk.shape[0] - 8
        own[k * size : (k + 1) * size] = chunk[:size]
        spots[k] = chunk[size:].astype(jnp.int32)


def join(chunks):
    size = chunks[0].shape[0] - 8
    return pl.pallas_call(
        join_kernel,
        out_shape=[
            jax.ShapeDtypeStruct((len(chunks) * size, LANES), jnp.float32),
            jax.ShapeDtypeStruct((len(chunks), 8, LANES), jnp.int32),
        ],
        in_specs=[VMEM] * len(chunks),
        out_specs=[VMEM] * 2,
        compiler_params=pltpu.CompilerParams(vmem_limit_bytes=14 * 2**20),
        cost_estimate=pl.CostEstimate(flops=0, bytes_accessed=2**16, transcendentals=0),
    )(*chunks)


def on_device(t_amps, v_tiles, v_where):
    cols = lax.axis_size("col")
    rows_axis = lax.axis_size("row")
    held, slots = v_tiles.shape[0], v_tiles.shape[3]
    pair = slots // cols
    rows = pair * HALF
    blocks = rows_axis // GROUP
    ranks = [
        [2 * (GROUP * m + (m.bit_count() + odd) % 2) + x for m in range(blocks // 2) for x in range(2)]
        for odd in range(2)
    ]
    row = lax.axis_index("row")
    place = jnp.stack(
        [lax.axis_index("col"), lax.axis_index("layer"), row // 2 % GROUP, row // (2 * GROUP) * 2]
    )

    def send(share, to, axis="col", size=cols):
        return lax.ppermute(share, axis, [(i, to(i)) for i in range(size)])

    def send_t(t_block):
        return send(t_block, lambda i: i ^ 2, "row", rows_axis)

    planes = [
        [(2 * z + x) * cols + c for x in range(2) for c in range(cols)] for z in range(rows_axis // 2)
    ]
    parts = pack(v_tiles, v_where, cols)
    parts = lax.all_to_all(parts, ("row", "col"), 0, 0, tiled=True, axis_index_groups=planes)
    chunks = sort(place, parts, blocks // 2)

    def send_m(chunk, k):
        return send(chunk, lambda i: i ^ (2 * GROUP * k) ^ (2 * (k.bit_count() % 2)), "row", rows_axis)

    own, spots = join([chunks[0]] + [send_m(chunks[k], k) for k in range(1, blocks // 2)])
    spots = spots[:, : 2 * GROUP, :slots].reshape(blocks * GROUP, slots)

    def up(i):
        return (i + 2) % cols

    def down(i):
        return (i - 2) % cols

    def across(i):
        return i ^ 1

    def add(sums, held, *shares):
        return contract(sums, place, spots, held, shares, pair)

    half, middle = own.shape[0] // 2, blocks // 2
    partner = send(own, across)
    below = send(own, up)
    above = send(own, down)
    tiles = {0: prepare(t_amps)}
    sums = add(None, tiles, ((0, 0, 0), own))
    sums, t_other = lax.optimization_barrier((sums, t_amps))
    t_other = send_t(t_other)
    sums, partner, below, above = lax.optimization_barrier((sums, partner, below, above))
    far_low = send(below[:half], up)
    far_high = send(above[half:], down)
    partner_below = send(partner, up)
    partner_above = send(partner, down)
    near = [((0, 0, 0), own), ((0, 0, 1), partner), ((0, -2, 0), below), ((0, 2, 0), above)]
    sums = add(sums, tiles, *near[1:])
    sums, far_low, far_high = lax.optimization_barrier((sums, far_low, far_high))
    partner_far_low = send(far_low, across)
    partner_far_high = send(far_high, across)
    other = {1: prepare(t_other)}
    sums = add(sums, other, *near)
    both = {**tiles, **other}
    sums = add(sums, both, ((0, 4, 0), far_low), ((middle, 4, 0), far_high))
    sums = add(sums, both, ((0, -2, 1), partner_below), ((0, 2, 1), partner_above))
    sums = add(sums, both, ((0, 4, 1), partner_far_low), ((middle, 4, 1), partner_far_high))

    sums = sums[0] + lax.ppermute(sums[1], "layer", [(0, 1), (1, 0)])
    sums = lax.all_to_all(sums, "row", 0, 0, tiled=True, axis_index_groups=ranks)
    return jnp.sum(sums, axis=0)


def solution(mesh):
    return jax.shard_map(
        on_device,
        mesh=mesh,
        in_specs=(
            P("col", ("row", "layer")),
            P("col", "layer", "row", None, None),
            P("col", "layer", "row", None),
        ),
        out_specs=P("col", ("row", "layer")),
        check_vma=False,
    )
```

```python
import jax
import jax.numpy as jnp
from jax import lax
from jax.experimental import pallas as pl
from jax.experimental.pallas import tpu as pltpu
from jax.sharding import PartitionSpec as P

TILE = 64
AB_DEV = 128
LANES = 128
GROUP = 2
HALF = TILE // 2
VMEM = pl.BlockSpec(memory_space=pltpu.VMEM)
SMEM = pl.BlockSpec(memory_space=pltpu.SMEM)
ANYWHERE = pl.BlockSpec(memory_space=pl.ANY)


def split_rows(x):
    hi = x.astype(jnp.bfloat16)
    return hi, (x - hi.astype(jnp.float32)).astype(jnp.bfloat16)


def pack_kernel(spots_in, lists_in, out, spots, lists, arrived):
    copies = [pltpu.make_async_copy(spots_in, spots, arrived.at[0])]
    for b in range(lists.shape[0]):
        copies.append(pltpu.make_async_copy(lists_in.at[b], lists.at[b], arrived.at[1 + b]))
    for copy in copies:
        copy.start()
    copies[0].wait()
    held, slots = spots.shape
    cols = out.shape[0] // held
    pair = slots // cols
    rows = pair * HALF
    lane = lax.broadcasted_iota(jnp.int32, (8, LANES), 1)
    for b in range(held):
        copies[1 + b].wait()
        row = jnp.zeros((8, LANES), jnp.float32)
        for s in range(slots):
            row = jnp.where(lane == s, spots[b, s].astype(jnp.float32), row)
        for c in range(cols):
            for p in range(pair):
                s = c * pair + p
                out[b * cols + c, p * HALF : (p + 1) * HALF] = lists[b, s // 8, pl.ds(s % 8, HALF, stride=8), :]
            out[b * cols + c, rows:] = row


def pack(v_tiles, v_where, cols):
    held, slots = v_tiles.shape[0], v_tiles.shape[3]
    lists = v_tiles.reshape(held, slots // 8, 8, HALF, LANES).transpose(0, 1, 3, 2, 4)
    lists = lists.reshape(held, slots // 8, HALF * 8, LANES)
    return pl.pallas_call(
        pack_kernel,
        out_shape=jax.ShapeDtypeStruct((held * cols, slots // cols * HALF + 8, LANES), jnp.float32),
        in_specs=[ANYWHERE, ANYWHERE],
        out_specs=VMEM,
        scratch_shapes=[
            pltpu.SMEM((held, slots), jnp.int32),
            pltpu.VMEM(lists.shape, jnp.float32),
            pltpu.SemaphoreType.DMA((1 + held,)),
        ],
        compiler_params=pltpu.CompilerParams(vmem_limit_bytes=60 * 2**20),
        cost_estimate=pl.CostEstimate(flops=0, bytes_accessed=2**20, transcendentals=0),
    )(v_where.reshape(held, slots), lists)


def prepare_kernel(*refs):
    *halves, t_tiles = refs
    row = lax.broadcasted_iota(jnp.int32, (LANES, 2 * LANES), 0)
    col = lax.broadcasted_iota(jnp.int32, (LANES, 2 * LANES), 1)
    source = (col // LANES) * TILE + 2 * (col % HALF) + (col % TILE) // HALF
    pick = (row == source).astype(jnp.bfloat16)
    for at in range(halves[0].shape[1] // LANES):
        split = [split_rows(half[:, at * LANES : (at + 1) * LANES]) for half in halves]
        rows = jnp.concatenate([hi for hi, _ in split] + [lo for _, lo in split], axis=0)
        both = jnp.dot(rows, pick, preferred_element_type=jnp.float32).astype(jnp.bfloat16)
        t_tiles[2 * at] = both[:, :LANES]
        t_tiles[2 * at + 1] = both[:, LANES:]


def prepare(*halves):
    ij, cd = sum(half.shape[0] for half in halves), halves[0].shape[1]
    return pl.pallas_call(
        prepare_kernel,
        out_shape=jax.ShapeDtypeStruct((cd // TILE, 2 * ij, LANES), jnp.bfloat16),
        in_specs=[VMEM] * len(halves),
        out_specs=VMEM,
        compiler_params=pltpu.CompilerParams(vmem_limit_bytes=14 * 2**20),
        cost_estimate=pl.CostEstimate(flops=2 * 2 * ij * cd * 2 * LANES, bytes_accessed=3 * 2**20, transcendentals=0),
    )(*halves)


def slot_rows(v, spot):
    lane_half = lax.broadcasted_iota(jnp.int32, (HALF, LANES), 1) // TILE
    safe = jnp.maximum(spot, 0)
    ab_half = safe & 1
    ab_pair = (safe >> 1) & 1
    swapped = pltpu.roll(v, TILE, 1)
    upper = ab_half == 1
    keep = (lane_half == ab_half) & (spot >= 0)
    hi_e, lo_e = split_rows(jnp.where(keep, jnp.where(upper, swapped, v), 0.0))
    hi_o, lo_o = split_rows(jnp.where(keep, jnp.where(upper, v, swapped), 0.0))
    rows = jnp.concatenate([hi_e, hi_o, lo_e, lo_o], axis=0)
    none = jnp.zeros_like(rows)
    return jnp.concatenate([jnp.where(ab_pair == 0, rows, none), jnp.where(ab_pair == 1, rows, none)], axis=1)


def contract_kernel(sources, offsets, fresh, pair, group, *refs):
    count, blocks_held = len(sources), len(offsets)
    place, spots = refs[:2]
    t_tiles = refs[2 : 2 + blocks_held]
    shares = refs[2 + blocks_held : 2 + blocks_held + count]
    rest = refs[2 + blocks_held + count :]
    sums = None if fresh else rest[0]
    out = rest[-1]
    layer = place[1]
    blocks, ij = out.shape[1:3]
    rows = pair * HALF
    cols = spots.shape[1] // pair
    columns = [((place[0] + shift) & (cols - 1)) ^ flip for _, shift, flip in sources]
    members = [place[2] ^ offset for offset in offsets]
    for block in range(blocks):
        used = [
            n for n in range(count)
            if sources[n][0] <= block < sources[n][0] + shares[n].shape[0] // (group * rows)
        ]
        total = None
        for n in used:
            for held in range(blocks_held):
                first = pl.multiple_of(((block - sources[n][0]) * group + members[held]) * rows, rows)
                left, right = [], []
                for p in range(pair):
                    spot = spots[block * group + members[held], columns[n] * pair + p]
                    left.append(t_tiles[held][jnp.maximum(spot, 0) >> 2])
                    right.append(slot_rows(shares[n][pl.ds(first + p * HALF, HALF), :], spot))
                part = jnp.dot(
                    jnp.concatenate(left, axis=1),
                    jnp.concatenate(right, axis=0),
                    preferred_element_type=jnp.float32,
                )
                total = part if total is None else total + part
        total = total[:ij] + total[ij:]
        mine = total[:, :LANES]
        other = total[:, LANES:]
        to = place[3] ^ block
        if sums is not None:
            mine = mine + sums[layer, to]
            other = other + sums[1 - layer, to]
        out[layer, to] = mine
        out[1 - layer, to] = other


def contract(sums, place, spots, held, shares, pair):
    group = GROUP
    blocks = spots.shape[0] // group
    ij = next(iter(held.values())).shape[1] // 2
    sources = tuple(source for source, _ in shares)
    offsets = tuple(held)
    given = [place, spots, *held.values(), *(share for _, share in shares)]
    specs = [SMEM, SMEM] + [VMEM] * (len(given) - 2)
    if sums is not None:
        given.append(sums)
        specs.append(VMEM)

    def kernel(*refs):
        contract_kernel(sources, offsets, sums is None, pair, group, *refs)

    return pl.pallas_call(
        kernel,
        out_shape=jax.ShapeDtypeStruct((2, blocks, ij, LANES), jnp.float32),
        in_specs=specs,
        out_specs=VMEM,
        input_output_aliases={} if sums is None else {len(given) - 1: 0},
        compiler_params=pltpu.CompilerParams(vmem_limit_bytes=14 * 2**20),
        cost_estimate=pl.CostEstimate(
            flops=2**12,
            bytes_accessed=2**10,
            transcendentals=0,
        ),
    )(*given)


def sort_kernel(place, parts, *chunks):
    cols = parts.shape[0] // 2
    rows = parts.shape[1] - 8
    for k in range(len(chunks)):
        first = ((place[3] >> 1) ^ k) * GROUP
        at = lax.broadcasted_iota(jnp.int32, (8, LANES), 0)
        spots = jnp.zeros((8, LANES), jnp.float32)
        for x in range(2):
            for e in range(GROUP):
                n, source = x * GROUP + e, x * cols + first + e
                chunks[k][n * rows : (n + 1) * rows] = parts[source, :rows]
                spots = jnp.where(at == n, parts[source, rows:], spots)
        chunks[k][2 * GROUP * rows :] = spots


def sort(place, parts, count):
    rows = parts.shape[1] - 8
    return pl.pallas_call(
        sort_kernel,
        out_shape=[jax.ShapeDtypeStruct((2 * GROUP * rows + 8, LANES), jnp.float32)] * count,
        in_specs=[SMEM, VMEM],
        out_specs=[VMEM] * count,
        compiler_params=pltpu.CompilerParams(vmem_limit_bytes=14 * 2**20),
        cost_estimate=pl.CostEstimate(flops=0, bytes_accessed=2**16, transcendentals=0),
    )(place, parts)


def join_kernel(*refs):
    *chunks, rest, spots = refs
    size = chunks[0].shape[0] - 8
    for k, chunk in enumerate(chunks):
        if k:
            rest[(k - 1) * size : k * size] = chunk[:size]
        spots[k] = chunk[size:].astype(jnp.int32)


def join(chunks):
    size = chunks[0].shape[0] - 8
    return pl.pallas_call(
        join_kernel,
        out_shape=[
            jax.ShapeDtypeStruct(((len(chunks) - 1) * size, LANES), jnp.float32),
            jax.ShapeDtypeStruct((len(chunks), 8, LANES), jnp.int32),
        ],
        in_specs=[VMEM] * len(chunks),
        out_specs=[VMEM] * 2,
        compiler_params=pltpu.CompilerParams(vmem_limit_bytes=14 * 2**20),
        cost_estimate=pl.CostEstimate(flops=0, bytes_accessed=2**16, transcendentals=0),
    )(*chunks)


def on_device(t_amps, v_tiles, v_where):
    cols = lax.axis_size("col")
    rows_axis = lax.axis_size("row")
    held, slots = v_tiles.shape[0], v_tiles.shape[3]
    pair = slots // cols
    rows = pair * HALF
    blocks = rows_axis // GROUP
    ranks = [
        [2 * (GROUP * m + (m.bit_count() + odd) % 2) + x for m in range(blocks // 2) for x in range(2)]
        for odd in range(2)
    ]
    row = lax.axis_index("row")
    place = jnp.stack(
        [lax.axis_index("col"), lax.axis_index("layer"), row // 2 % GROUP, row // (2 * GROUP) * 2]
    )

    def send(share, to, axis="col", size=cols):
        return lax.ppermute(share, axis, [(i, to(i)) for i in range(size)])

    def send_t(t_block):
        return send(t_block, lambda i: i ^ 2, "row", rows_axis)

    planes = [
        [(2 * z + x) * cols + c for x in range(2) for c in range(cols)] for z in range(rows_axis // 2)
    ]
    parts = pack(v_tiles, v_where, cols)
    parts = lax.all_to_all(parts, ("row", "col"), 0, 0, tiled=True, axis_index_groups=planes)
    chunks = sort(place, parts, blocks // 2)

    def send_m(chunk, k):
        return send(chunk, lambda i: i ^ (2 * GROUP * k) ^ (2 * (k.bit_count() % 2)), "row", rows_axis)

    def up(i):
        return (i + 2) % cols

    def down(i):
        return (i - 2) % cols

    def across(i):
        return i ^ 1

    first = chunks[0]
    others = [send_m(chunks[k], k) for k in range(1, blocks // 2)]
    first_partner, first_below, first_above = send(first, across), send(first, up), send(first, down)
    first_far = send(first_below, up)
    first_partner_below, first_partner_above = send(first_partner, up), send(first_partner, down)
    own, spots = join([first] + others)
    own, first_above, first_far, first_partner_below, first_partner_above = lax.optimization_barrier(
        (own, first_above, first_far, first_partner_below, first_partner_above)
    )
    spots = spots[:, : 2 * GROUP, :slots].reshape(blocks * GROUP, slots)

    def add(sums, held, *shares):
        return contract(sums, place, spots, held, shares, pair)

    half, low, middle = own.shape[0] // 2, 2, 1 + blocks // 2
    partner = send(own, across)
    below = send(own, up)
    above = send(own, down)
    tiles = {0: prepare(t_amps)}
    sums = add(None, tiles, ((0, 0, 0), first), ((low, 0, 0), own))
    sums, t_other = lax.optimization_barrier((sums, t_amps))
    t_other = send_t(t_other)
    sums, partner, below, above = lax.optimization_barrier((sums, partner, below, above))
    far_low = send(below[:half], up)
    far_high = send(above[half:], down)
    partner_below = send(partner, up)
    partner_above = send(partner, down)
    near = [
        ((0, 0, 0), first),
        ((low, 0, 0), own),
        ((0, 0, 1), first_partner),
        ((low, 0, 1), partner),
        ((0, -2, 0), first_below),
        ((low, -2, 0), below),
        ((0, 2, 0), first_above),
        ((low, 2, 0), above),
    ]
    sums = add(sums, tiles, *near[2:])
    sums, far_low, far_high, first_far = lax.optimization_barrier((sums, far_low, far_high, first_far))
    partner_far_low = send(far_low, across)
    partner_far_high = send(far_high, across)
    first_partner_far = send(first_far, across)
    other = {1: prepare(t_other)}
    sums = add(sums, other, *near)
    both = {**tiles, **other}
    sums = add(sums, both, ((0, 4, 0), first_far), ((low, 4, 0), far_low), ((middle, 4, 0), far_high))
    sums = add(
        sums,
        both,
        ((0, -2, 1), first_partner_below),
        ((low, -2, 1), partner_below),
        ((0, 2, 1), first_partner_above),
        ((low, 2, 1), partner_above),
    )
    sums = add(
        sums,
        both,
        ((0, 4, 1), first_partner_far),
        ((low, 4, 1), partner_far_low),
        ((middle, 4, 1), partner_far_high),
    )

    sums = sums[0] + lax.ppermute(sums[1], "layer", [(0, 1), (1, 0)])
    sums = lax.all_to_all(sums, "row", 0, 0, tiled=True, axis_index_groups=ranks)
    return jnp.sum(sums, axis=0)


def solution(mesh):
    return jax.shard_map(
        on_device,
        mesh=mesh,
        in_specs=(
            P("col", ("row", "layer")),
            P("col", "layer", "row", None, None),
            P("col", "layer", "row", None),
        ),
        out_specs=P("col", ("row", "layer")),
        check_vma=False,
    )
```
